128 devices in a mesh: ctx: 16 (over z, x), tp: 8 (over y, core).
Axes of the slice: x: 4, y: 4, z: 4, core: 2. Of those that a mesh axis runs over, the one named last changes fastest.
Arguments:
- qkv: bfloat16 [3, 8192, 4096], P(None, ('ctx', 'tp')), may hold values from -6 to 6
- residues: float32 [4096, 16], P('tp'), may hold values from -2 to 2
- spans: float32 [4096, 16], P('tp'), may hold values from 20 to 40960
- skip: float32 [4096], P('tp'), may hold values from -3 to 3
Outputs:
- gated: bfloat16 [4096, 8192], P('tp', 'ctx')
The draws below stay inside these ranges and needn't reach their ends.
All inputs are finite; a program needn't handle non-finite values.
Results may differ from the reference program's by a relative error of at most 0.00205.
Values may be sent and summed in bfloat16 or wider, within the bound.
No kernel may reach another device: no remote copies, remote signals or barrier semaphores. Data moves between devices by JAX's collectives and lax.ppermute only.
A program may use at most 192 MiB of HBM per device.

```python
import math
import jax
import jax.numpy as jnp
from jax import lax

CH = 4096
ORDER = 16
TOKENS = 8192


def block_levels(rng, extent, cuts, smallest, high):
    def one(axis_at, shards_of):
        draws = jax.random.uniform(jax.random.fold_in(jax.random.fold_in(rng, 6), axis_at), (shards_of,), jnp.float32, smallest / len(cuts), high / len(cuts))
        return jnp.repeat(jnp.exp(draws), extent[axis_at] // shards_of).reshape((-1,) + (1,) * (len(extent) - axis_at - 1))

    loudness = one(*cuts[0])
    for cut in cuts[1:]:
        loudness = loudness * one(*cut)
    return loudness


def centred(key, extent, deviation, bound, pieces=(), kind=jnp.bfloat16):
    factor_of = block_levels(key, extent, pieces, -0.22, 0.18) if pieces else 1.0
    values = jax.random.normal(key, extent, jnp.float32) * deviation * factor_of
    return jnp.minimum(jnp.maximum(values, -bound), bound).astype(kind)


def setup_inputs(seed: int = 0) -> dict:
    streams_of = jax.random.split(jax.random.key(seed), 5)
    qkv = centred(streams_of[0], (3, TOKENS, CH), 1.0, 6.0, ((1, 128),))
    residues = centred(streams_of[1], (CH, ORDER), 0.35, 2.0, ((0, 8),), jnp.float32)
    spans = jnp.clip(jnp.exp(math.log(40960.0) - 7.624619 * jax.random.uniform(streams_of[2], (CH, ORDER), jnp.float32) ** block_levels(streams_of[2], (CH, ORDER), ((0, 8),), -0.2, 0.2)), 20.0, 40960.0)
    skip = centred(streams_of[3], (CH,), 0.7, 3.0, ((0, 8),), jnp.float32)
    return dict(qkv=qkv, residues=residues, spans=spans, skip=skip)


def conv_block(inputs):
    scaled, rates, drive = inputs
    times = jnp.arange(TOKENS, dtype=jnp.float32)
    filt = lax.optimization_barrier(jnp.sum(scaled[:, :, None] * jnp.exp(-rates[:, :, None] * times[None, None, :]), axis=1))
    spectrum = jnp.fft.rfft(drive, n=2 * TOKENS) * jnp.fft.rfft(filt, n=2 * TOKENS)
    return jnp.fft.irfft(spectrum, n=2 * TOKENS)[:, :TOKENS]

def reference(qkv, residues, spans, skip):
    queries = qkv[0].astype(jnp.float32).T
    drive = (qkv[1].astype(jnp.float32) * qkv[2].astype(jnp.float32)).T
    rates = 1.0 / spans
    scaled = residues * jnp.sqrt(rates)
    group = 32 if CH % 32 == 0 else CH
    blocks = CH // group
    conv = lax.map(conv_block, (scaled.reshape(blocks, group, ORDER), rates.reshape(blocks, group, ORDER), drive.reshape(blocks, group, TOKENS)))
    conv = conv.reshape(CH, TOKENS)
    return (queries * (conv + skip[:, None] * drive)).astype(jnp.bfloat16)
```

```python
import functools

import jax
import jax.numpy as jnp
from jax import lax
from jax.experimental import pallas as pl
from jax.experimental.pallas import tpu as pltpu
from jax.sharding import PartitionSpec as P

F32 = jnp.float32
BF16 = jnp.bfloat16
SUBS = 8
LANES = 128


def encode(drive):
    scaled = drive * 1024.0
    size = jnp.abs(scaled)
    square = scaled * scaled
    fourth = square * square
    code = jnp.where(size >= 1.0, fourth * fourth, size)
    return jnp.where(scaled < 0.0, -code, code).astype(BF16)


def decode(code):
    code = code.astype(F32)
    size = jnp.abs(code)
    half = lax.rsqrt(jnp.maximum(size, 1.0))
    quarter = lax.rsqrt(half)
    root = quarter * lax.rsqrt(quarter)
    drive = jnp.where(size >= 1.0, root, size) * (1.0 / 1024.0)
    return jnp.where(code < 0.0, -drive, drive)


def encode_kernel(qkv_ref, code_ref, query_ref):
    drive = qkv_ref[1].astype(F32) * qkv_ref[2].astype(F32)
    code_ref[0] = encode(drive)
    query_ref[0] = qkv_ref[0]


def wide(ref, mode, lanes):
    return jnp.broadcast_to(ref[mode : mode + 1, lanes], (SUBS, LANES))


def state_kernel(modes, code_ref, decay_ref, tail_ref, drive_ref, sub_ref, block_ref):
    subs, steps, channels = code_ref.shape
    for sub in range(subs):
        rows = pl.ds(sub * steps, steps)
        for group in range(channels // LANES):
            lanes = pl.ds(group * LANES, LANES)
            drive_ref[group, rows, :] = decode(code_ref[sub, :, lanes])
    for group in range(channels // LANES):
        lanes = pl.ds(group * LANES, LANES)
        decay = [wide(decay_ref, mode, lanes) for mode in range(modes)]

        def step(i, states):
            x = drive_ref[group, pl.ds(i, SUBS, stride=steps), :]
            return [states[m] * decay[m] + x for m in range(modes)]

        zero = jnp.zeros((SUBS, LANES), F32)
        states = lax.fori_loop(0, steps, step, [zero] * modes, unroll=8)
        for mode in range(modes):
            sub_ref[mode, :, lanes] = states[mode]
            block_ref[mode : mode + 1, lanes] = jnp.sum(
                states[mode] * tail_ref[mode, :, lanes], axis=0, keepdims=True
            )


def local_kernel(modes, drive_ref, sub_ref, decay_ref, step_decay_ref, weight_ref, skip_ref, out_ref):
    groups, tokens, _ = drive_ref.shape
    steps = tokens // SUBS
    for group in range(groups):
        lanes = pl.ds(group * LANES, LANES)
        decay = [wide(decay_ref, mode, lanes) for mode in range(modes)]
        weight = [wide(weight_ref, mode, lanes) for mode in range(modes)]
        row = lax.broadcasted_iota(jnp.int32, (SUBS, LANES), 0)
        first = []
        for mode in range(modes):
            held = sub_ref[mode, :, lanes]
            factor = wide(step_decay_ref, mode, lanes)
            shift = 1
            while shift < SUBS:
                moved = jnp.where(row >= shift, pltpu.roll(held, shift, 0), 0.0)
                held = held + factor * moved
                factor = factor * factor
                shift *= 2
            first.append(jnp.where(row >= 1, pltpu.roll(held, 1, 0), 0.0))
        skip = jnp.broadcast_to(skip_ref[0:1, lanes], (SUBS, LANES))

        def step(i, states):
            at = pl.ds(i, SUBS, stride=steps)
            x = drive_ref[group, at, :]
            states = [states[m] * decay[m] + x for m in range(modes)]
            parts = [states[m] * weight[m] for m in range(modes)] + [skip * x]
            while len(parts) > 1:
                parts = [parts[j] + parts[j + 1] if j + 1 < len(parts) else parts[j] for j in range(0, len(parts), 2)]
            out_ref[group, at, :] = parts[0]
            return states

        lax.fori_loop(0, steps, step, first, unroll=4)


def final_kernel(modes, local_ref, query_ref, carry_ref, start_ref, decay_ref, out_ref, sum_ref):
    groups, tokens, _ = local_ref.shape
    steps = tokens // SUBS
    for group in range(groups):
        lanes = pl.ds(group * LANES, LANES)
        decay = [wide(decay_ref, mode, lanes) for mode in range(modes)]
        first = [start_ref[mode, :, lanes] * wide(carry_ref, mode, lanes) for mode in range(modes)]

        def step(i, states):
            at = pl.ds(i, SUBS, stride=steps)
            parts = [local_ref[group, at, :]] + states
            while len(parts) > 1:
                parts = [parts[j] + parts[j + 1] if j + 1 < len(parts) else parts[j] for j in range(0, len(parts), 2)]
            sum_ref[group, at, :] = parts[0]
            return [states[m] * decay[m] for m in range(modes)]

        lax.fori_loop(0, steps, step, first, unroll=8)
        for tile in range(tokens // LANES):
            rows = pl.ds(tile * LANES, LANES)
            gated = sum_ref[group, rows, :] * query_ref[rows, lanes].astype(F32)
            out_ref[pl.ds(group * LANES, LANES), rows] = gated.T.astype(BF16)


def per_device(qkv, residues, spans, skip):
    _, span_tokens, all_channels = qkv.shape
    devices = lax.axis_size("tp")
    channels, modes = residues.shape
    tokens = devices * span_tokens
    steps = tokens // SUBS
    groups = channels // LANES
    vmem = pl.BlockSpec(memory_space=pltpu.VMEM)
    params = pltpu.CompilerParams(vmem_limit_bytes=32 * 1024 * 1024)

    code, query = pl.pallas_call(
        encode_kernel,
        grid=(devices,),
        in_specs=[pl.BlockSpec((3, span_tokens, channels), lambda j: (0, 0, j))],
        out_specs=[pl.BlockSpec((1, span_tokens, channels), lambda j: (j, 0, 0))] * 2,
        out_shape=[jax.ShapeDtypeStruct((devices, span_tokens, channels), BF16)] * 2,
    )(qkv)
    code = lax.all_to_all(code, "tp", 0, 0)
    query = lax.all_to_all(query, "tp", 0, 0).reshape(tokens, channels)

    rates = 1.0 / spans.T
    weight = residues.T * jnp.sqrt(rates)
    decay = jnp.exp(-rates)
    sub_index = jnp.arange(SUBS, dtype=F32)[None, :, None]
    tail = jnp.exp(-rates[:, None, :] * (steps * (SUBS - 1 - sub_index)))
    start = weight[:, None, :] * jnp.exp(-rates[:, None, :] * (steps * sub_index + 1.0))
    step_decay = jnp.exp(-rates * steps)

    drive, subs, block = pl.pallas_call(
        functools.partial(state_kernel, modes),
        in_specs=[vmem] * 3,
        out_specs=[vmem] * 3,
        out_shape=[
            jax.ShapeDtypeStruct((groups, tokens, LANES), F32),
            jax.ShapeDtypeStruct((modes, SUBS, channels), F32),
            jax.ShapeDtypeStruct((modes, channels), F32),
        ],
        compiler_params=params,
        cost_estimate=pl.CostEstimate(flops=40_000_000, bytes_accessed=2_000_000, transcendentals=0),
    )(code, decay, tail)

    local = pl.pallas_call(
        functools.partial(local_kernel, modes),
        in_specs=[vmem] * 6,
        out_specs=vmem,
        out_shape=jax.ShapeDtypeStruct((groups, tokens, LANES), F32),
        compiler_params=params,
        cost_estimate=pl.CostEstimate(flops=80_000_000, bytes_accessed=2_000_000, transcendentals=0),
    )(drive, subs, decay, step_decay, weight, skip.reshape(1, channels))

    blocks = lax.axis_size("ctx")
    cols = 4
    place = lax.axis_index("ctx")
    col = place % cols
    row = place // cols

    def swapped(value, bits):
        return lax.ppermute(value, "ctx", [(i, i ^ bits) for i in range(blocks)])

    def power(count):
        count = jnp.asarray(count)
        factor = jnp.exp(-rates * jnp.maximum(count, 0).astype(F32))
        return jnp.where(count >= 0, factor, 0.0)

    before = jnp.zeros_like(block)
    total = power(tokens * (cols - 1 - col)) * block
    for k in range(1, cols):
        other = swapped(block, k)
        before = before + power(tokens * (col - 1 - (col ^ k))) * other
        total = total + power(tokens * (cols - 1 - (col ^ k))) * other
    carry = jnp.zeros_like(block)
    for k in range(1, blocks // cols):
        other = swapped(total, k * cols)
        carry = carry + power(tokens * cols * (row - 1 - (row ^ k))) * other
    carry = before + power(tokens * col) * carry

    return pl.pallas_call(
        functools.partial(final_kernel, modes),
        in_specs=[vmem] * 5,
        out_specs=vmem,
        out_shape=jax.ShapeDtypeStruct((channels, tokens), BF16),
        scratch_shapes=[pltpu.VMEM((groups, tokens, LANES), F32)],
        compiler_params=params,
        cost_estimate=pl.CostEstimate(flops=40_000_000, bytes_accessed=2_000_000, transcendentals=0),
    )(local, query, carry, start, decay)


def solution(mesh):
    return jax.shard_map(
        per_device,
        mesh=mesh,
        in_specs=(P(None, ("ctx", "tp"), None), P("tp", None), P("tp", None), P("tp")),
        out_specs=P("tp", "ctx"),
        check_vma=False,
    )
```

```python
import functools

import jax
import jax.numpy as jnp
from jax import lax
from jax.experimental import pallas as pl
from jax.experimental.pallas import tpu as pltpu
from jax.sharding import PartitionSpec as P

F32 = jnp.float32
BF16 = jnp.bfloat16
SUBS = 8
LANES = 128
SCALE = 1024.0


def encode(scaled):
    size = jnp.maximum(jnp.abs(scaled), 1.0)
    square = size * size
    return (scaled * (square * square * square * size)).astype(BF16)


def decode(code):
    code = code.astype(F32)
    half = lax.rsqrt(jnp.maximum(jnp.abs(code), 1.0))
    eighth = lax.rsqrt(lax.rsqrt(half))
    return code * (half * eighth * eighth * eighth)


def open_kernel(qkv_ref, own_ref, other_ref, query_own_ref, query_other_ref, held_ref, held_sem, query_sem):
    chips, tokens, width = own_ref.shape
    place = lax.axis_index("tp")
    chip, core = place // 2, place % 2

    def fetch(k):
        lanes = pl.ds(pl.multiple_of((chip ^ k) * 2 * width, 2 * width), 2 * width)
        return pltpu.make_async_copy(qkv_ref.at[pl.ds(1, 2), :, lanes], held_ref.at[k], held_sem.at[k])

    def pass_on(k, flip):
        lanes = pl.ds(pl.multiple_of((place ^ (2 * k + flip)) * width, width), width)
        out_ref = (query_own_ref, query_other_ref)[flip]
        return pltpu.make_async_copy(qkv_ref.at[0, :, lanes], out_ref.at[k], query_sem.at[2 * k + flip])

    for k in range(chips):
        fetch(k).start()
    for k in range(chips):
        for flip in range(2):
            pass_on(k, flip).start()
    for k in range(chips):
        fetch(k).wait()
        for flip, out_ref in ((0, own_ref), (1, other_ref)):
            half = pl.ds(pl.multiple_of((core ^ flip) * width, width), width)
            scaled = held_ref[k, 0, :, half].astype(F32) * held_ref[k, 1, :, half].astype(F32) * SCALE
            out_ref[k] = encode(scaled)
    for k in range(chips):
        for flip in range(2):
            pass_on(k, flip).wait()


def across_core(value):
    return lax.ppermute(value, "tp", [(i, i ^ 1) for i in range(lax.axis_size("tp"))])


def across_chips(value, k):
    return lax.ppermute(value, "tp", [(i, i ^ 2 * k) for i in range(lax.axis_size("tp"))])


def wide(ref, mode, lanes):
    return jnp.broadcast_to(ref[mode : mode + 1, lanes], (SUBS, LANES))


def state_kernel(modes, code_ref, decay_ref, tail_ref, drive_ref, sub_ref, block_ref):
    chips, _, steps, channels = code_ref.shape
    place = lax.axis_index("tp")
    for sub in range(2 * chips):
        k, flip = (place // 2) ^ (sub // 2), (place % 2) ^ (sub % 2)
        rows = pl.ds(sub * steps, steps)
        for group in range(channels // LANES):
            lanes = pl.ds(group * LANES, LANES)
            drive_ref[group, rows, :] = decode(code_ref[k, flip, :, lanes])
    for group in range(channels // LANES):
        lanes = pl.ds(group * LANES, LANES)
        decay = [wide(decay_ref, mode, lanes) for mode in range(modes)]

        def step(i, states):
            x = drive_ref[group, pl.ds(i, SUBS, stride=steps), :]
            return [states[m] * decay[m] + x for m in range(modes)]

        zero = jnp.zeros((SUBS, LANES), F32)
        states = lax.fori_loop(0, steps, step, [zero] * modes, unroll=8)
        for mode in range(modes):
            sub_ref[mode, :, lanes] = states[mode]
            block_ref[mode : mode + 1, lanes] = jnp.sum(
                states[mode] * tail_ref[mode, :, lanes], axis=0, keepdims=True
            )


def local_kernel(modes, begin, drive_ref, sub_ref, decay_ref, step_decay_ref, weight_ref, skip_ref, out_ref):
    groups, tokens, _ = out_ref.shape
    steps = tokens // SUBS
    for group in range(groups):
        lanes = pl.ds((begin + group) * LANES, LANES)
        decay = [wide(decay_ref, mode, lanes) for mode in range(modes)]
        weight = [wide(weight_ref, mode, lanes) for mode in range(modes)]
        row = lax.broadcasted_iota(jnp.int32, (SUBS, LANES), 0)
        first = []
        for mode in range(modes):
            held = sub_ref[mode, :, lanes]
            factor = wide(step_decay_ref, mode, lanes)
            shift = 1
            while shift < SUBS:
                moved = jnp.where(row >= shift, pltpu.roll(held, shift, 0), 0.0)
                held = held + factor * moved
                factor = factor * factor
                shift *= 2
            first.append(jnp.where(row >= 1, pltpu.roll(held, 1, 0), 0.0))
        skip = jnp.broadcast_to(skip_ref[0:1, lanes], (SUBS, LANES))

        def step(i, states):
            at = pl.ds(i, SUBS, stride=steps)
            x = drive_ref[begin + group, at, :]
            states = [states[m] * decay[m] + x for m in range(modes)]
            parts = [states[m] * weight[m] for m in range(modes)] + [skip * x]
            while len(parts) > 1:
                parts = [parts[j] + parts[j + 1] if j + 1 < len(parts) else parts[j] for j in range(0, len(parts), 2)]
            out_ref[group, at, :] = parts[0]
            return states

        lax.fori_loop(0, steps, step, first, unroll=4)


def final_kernel(modes, low_ref, high_ref, part_ref, carry_ref, start_ref, decay_ref, out_ref, sum_ref, query_ref):
    groups, tokens, _ = sum_ref.shape
    steps = tokens // SUBS
    place = lax.axis_index("tp")
    for sub in range(SUBS):
        query_ref[pl.ds(sub * steps, steps), :] = part_ref[(place // 2) ^ (sub // 2), (place % 2) ^ (sub % 2)]
    for group in range(groups):
        lanes = pl.ds(group * LANES, LANES)
        decay = [wide(decay_ref, mode, lanes) for mode in range(modes)]
        local_ref = (low_ref, high_ref)[group // (groups // 2)]
        first = [start_ref[mode, :, lanes] * wide(carry_ref, mode, lanes) for mode in range(modes)]

        def step(i, states):
            at = pl.ds(i, SUBS, stride=steps)
            parts = [local_ref[group % (groups // 2), at, :]] + states
            while len(parts) > 1:
                parts = [parts[j] + parts[j + 1] if j + 1 < len(parts) else parts[j] for j in range(0, len(parts), 2)]
            sum_ref[group, at, :] = parts[0]
            return [states[m] * decay[m] for m in range(modes)]

        lax.fori_loop(0, steps, step, first, unroll=8)
        for tile in range(tokens // LANES):
            rows = pl.ds(tile * LANES, LANES)
            gated = sum_ref[group, rows, :] * query_ref[rows, lanes].astype(F32)
            out_ref[pl.ds(group * LANES, LANES), rows] = gated.T.astype(BF16)


def per_device(qkv, residues, spans, skip):
    _, span_tokens, all_channels = qkv.shape
    devices = lax.axis_size("tp")
    channels, modes = residues.shape
    tokens = devices * span_tokens
    steps = tokens // SUBS
    groups = channels // LANES
    vmem = pl.BlockSpec(memory_space=pltpu.VMEM)
    params = pltpu.CompilerParams(vmem_limit_bytes=32 * 1024 * 1024)

    chips = devices // 2
    own, other, query_own, query_other = pl.pallas_call(
        open_kernel,
        in_specs=[pl.BlockSpec(memory_space=pl.ANY)],
        out_specs=[vmem] * 4,
        out_shape=[jax.ShapeDtypeStruct((n, span_tokens, channels), BF16) for n in [chips] * 4],
        scratch_shapes=[
            pltpu.VMEM((chips, 2, span_tokens, 2 * channels), BF16),
            pltpu.SemaphoreType.DMA((chips,)),
            pltpu.SemaphoreType.DMA((devices,)),
        ],
        compiler_params=params,
    )(qkv)
    code = jnp.stack([own, across_core(other)], 1)
    code = jnp.stack([code[0]] + [across_chips(code[k], k) for k in range(1, chips)])
    query = jnp.stack([query_own, across_core(query_other)], 1)
    code, query = lax.optimization_barrier((code, query))

    rates = 1.0 / spans.T
    weight = residues.T * jnp.sqrt(rates) * (1.0 / SCALE)
    decay = jnp.exp(-rates)
    sub_index = jnp.arange(SUBS, dtype=F32)[None, :, None]
    tail = jnp.exp(-rates[:, None, :] * (steps * (SUBS - 1 - sub_index)))
    start = weight[:, None, :] * jnp.exp(-rates[:, None, :] * (steps * sub_index + 1.0))
    step_decay = jnp.exp(-rates * steps)

    drive, subs, block = pl.pallas_call(
        functools.partial(state_kernel, modes),
        in_specs=[vmem] * 3,
        out_specs=[vmem] * 3,
        out_shape=[
            jax.ShapeDtypeStruct((groups, tokens, LANES), F32),
            jax.ShapeDtypeStruct((modes, SUBS, channels), F32),
            jax.ShapeDtypeStruct((modes, channels), F32),
        ],
        compiler_params=params,
        cost_estimate=pl.CostEstimate(flops=40_000_000, bytes_accessed=2_000_000, transcendentals=0),
    )(code, decay, tail)

    local = [
        pl.pallas_call(
            functools.partial(local_kernel, modes, begin),
            in_specs=[vmem] * 6,
            out_specs=vmem,
            out_shape=jax.ShapeDtypeStruct((groups // 2, tokens, LANES), F32),
            compiler_params=params,
            cost_estimate=pl.CostEstimate(flops=40_000_000, bytes_accessed=4_000_000, transcendentals=0),
        )(drive, subs, decay, step_decay, weight, skip.reshape(1, channels) * (1.0 / SCALE))
        for begin in (0, groups // 2)
    ]

    query = lax.optimization_barrier((query, block))[0]
    query = [query[0]] + [across_chips(query[k], k) for k in range(1, chips)]

    index = lax.axis_index("ctx")
    col, row = index % 4, index // 4

    def swapped(value, bits):
        return lax.ppermute(value, "ctx", [(i, i ^ bits) for i in range(lax.axis_size("ctx"))])

    def power(count):
        return jnp.exp(-rates * jnp.asarray(count).astype(F32))

    def join(before, total, upper, offset, span, bits, along=()):
        other, *along = lax.optimization_barrier((swapped(total, bits), *along))
        before = before + jnp.where(upper, power(offset), 0.0) * other
        whole = power(span)
        total = jnp.where(upper, whole * other + total, whole * total + other)
        return before, total, along

    before, total, along = join(jnp.zeros_like(block), block, col % 2 == 1, 0, tokens, 1, local[:1])
    local[:1] = along
    before, total, _ = join(before, total, col >= 2, tokens * (col % 2), 2 * tokens, 3)
    before, total, along = join(before, total, row % 2 == 1, tokens * col, 4 * tokens, 4, [query[1], query[3]])
    query[1], query[3] = along
    along = [query[2], local[1]]
    carry, _, along = join(before, total, row >= 2, tokens * (col + 4 * (row % 2)), 8 * tokens, 12, along)
    query[2], local[1] = along
    query = jnp.stack(query)

    return pl.pallas_call(
        functools.partial(final_kernel, modes),
        in_specs=[vmem] * 6,
        out_specs=vmem,
        out_shape=jax.ShapeDtypeStruct((channels, tokens), BF16),
        scratch_shapes=[pltpu.VMEM((groups, tokens, LANES), F32), pltpu.VMEM((tokens, channels), BF16)],
        compiler_params=params,
        cost_estimate=pl.CostEstimate(flops=40_000_000, bytes_accessed=2_000_000, transcendentals=0),
    )(*local, query, carry, start, decay)


def solution(mesh):
    return jax.shard_map(
        per_device,
        mesh=mesh,
        in_specs=(P(None, ("ctx", "tp"), None), P("tp", None), P("tp", None), P("tp")),
        out_specs=P("tp", "ctx"),
        check_vma=False,
    )
```

```python
import functools

import jax
import jax.numpy as jnp
from jax import lax
from jax.experimental import pallas as pl
from jax.experimental.pallas import tpu as pltpu
from jax.sharding import PartitionSpec as P

F32 = jnp.float32
BF16 = jnp.bfloat16
SUBS = 8
LANES = 128
SCALE = 1024.0
VMEM = pl.BlockSpec(memory_space=pltpu.VMEM)
PARAMS = pltpu.CompilerParams(vmem_limit_bytes=32 * 1024 * 1024)


def encode(scaled):
    size = jnp.maximum(jnp.abs(scaled), 1.0)
    square = size * size
    return (scaled * (square * square * square * size)).astype(BF16)


def decode(code):
    code = code.astype(F32)
    half = lax.rsqrt(jnp.maximum(jnp.abs(code), 1.0))
    eighth = lax.rsqrt(lax.rsqrt(half))
    return code * (half * eighth * eighth * eighth)


def open_kernel(qkv_ref, *refs):
    *code_refs, low_ref, high_ref = refs
    _, _, width = code_refs[0].shape
    place = lax.axis_index("tp")
    chips = len(code_refs)
    for k, code_ref in enumerate(code_refs):
        for flip in range(2):
            lanes = pl.ds(pl.multiple_of((place ^ (2 * k + flip)) * width, width), width)
            code_ref[flip] = encode(qkv_ref[1, :, lanes].astype(F32) * qkv_ref[2, :, lanes].astype(F32) * SCALE)
    for half, out_ref in enumerate((low_ref, high_ref)):
        for part in range(chips):
            out_ref[part] = qkv_ref[0, :, pl.ds((half * chips + part) * width, width)]


def across_core(value):
    return lax.ppermute(value, "tp", [(i, i ^ 1) for i in range(lax.axis_size("tp"))])


def across_chips(value, k):
    return lax.ppermute(value, "tp", [(i, i ^ 2 * k) for i in range(lax.axis_size("tp"))])


def across_blocks(value, bits):
    return lax.ppermute(value, "ctx", [(i, i ^ bits) for i in range(lax.axis_size("ctx"))])


def wide(ref, mode, lanes):
    return jnp.broadcast_to(ref[mode : mode + 1, lanes], (SUBS, LANES))


def total_of(parts):
    while len(parts) > 1:
        parts = [parts[j] + parts[j + 1] if j + 1 < len(parts) else parts[j] for j in range(0, len(parts), 2)]
    return parts[0]


def state_kernel(modes, code_ref, decay_ref, tail_ref, earlier_ref, drive_ref, sub_ref, block_ref):
    chips, tokens, channels = code_ref.shape
    steps = chips * tokens // SUBS
    chip = lax.axis_index("tp") // 2
    for source in range(chips):
        for group in range(channels // LANES):
            lanes = pl.ds(group * LANES, LANES)
            drive_ref[group, pl.ds(source * tokens, tokens), :] = decode(code_ref[chip ^ source, :, lanes])
    for group in range(channels // LANES):
        lanes = pl.ds(group * LANES, LANES)
        decay = [wide(decay_ref, mode, lanes) for mode in range(modes)]

        def step(i, states):
            x = drive_ref[group, pl.ds(i, SUBS, stride=steps), :]
            return [states[m] * decay[m] + x for m in range(modes)]

        zero = jnp.zeros((SUBS, LANES), F32)
        states = lax.fori_loop(0, steps, step, [zero] * modes, unroll=8)
        for mode in range(modes):
            sub_ref[mode, :, lanes] = states[mode]
            block_ref[mode : mode + 1, lanes] = earlier_ref[mode : mode + 1, lanes] + jnp.sum(
                states[mode] * tail_ref[mode, :, lanes], axis=0, keepdims=True
            )


def first_states(near, far, decay_32, core):
    row = lax.broadcasted_iota(jnp.int32, (SUBS, LANES), 0)
    odd = row % 2 == 1
    decay_64 = decay_32 * decay_32
    decay_128 = decay_64 * decay_64
    first = jnp.where(core == 0, near, far)
    second = jnp.where(core == 0, far, near)
    first_before, second_before = pltpu.roll(first, 1, 0), pltpu.roll(second, 1, 0)
    first_whole = first + decay_32 * first_before
    held = second + decay_32 * second_before + decay_64 * first_whole
    held = held + decay_128 * jnp.where(row >= 2, pltpu.roll(held, 2, 0), 0.0)
    held = held + decay_128 * decay_128 * jnp.where(row >= 4, pltpu.roll(held, 4, 0), 0.0)
    into = jnp.where(odd, pltpu.roll(held, 2, 0), pltpu.roll(held, 1, 0))
    into = jnp.where(row >= 2, into, 0.0)
    middle = decay_64 * into + jnp.where(odd, first_whole, pltpu.roll(first_whole, SUBS - 1, 0))
    first = jnp.where(odd, decay_32 * into + first_before, into)
    second = jnp.where(odd, decay_32 * middle + second_before, middle)
    return jnp.where(core == 0, first, second), jnp.where(core == 0, second, first)


def local_kernel(modes, begin, *refs):
    drive_refs, (near_ref, far_ref, decay_ref, step_decay_ref, weight_ref, skip_ref), out_refs = refs[:2], refs[2:8], refs[8:]
    groups, tokens, _ = out_refs[0].shape
    steps = tokens // SUBS
    core = lax.axis_index("tp") % 2
    for group in range(groups):
        lanes = pl.ds((begin + group) * LANES, LANES)
        decay = [wide(decay_ref, mode, lanes) for mode in range(modes)]
        weight = [wide(weight_ref, mode, lanes) for mode in range(modes)]
        skip = jnp.broadcast_to(skip_ref[0:1, lanes], (SUBS, LANES))
        starts = [
            first_states(near_ref[m, :, lanes], far_ref[m, :, lanes], wide(step_decay_ref, m, lanes), core)
            for m in range(modes)
        ]
        for part, (drive_ref, out_ref) in enumerate(zip(drive_refs, out_refs)):

            def step(i, states):
                at = pl.ds(i, SUBS, stride=steps)
                x = drive_ref[begin + group, at, :]
                states = [states[m] * decay[m] + x for m in range(modes)]
                out_ref[group, at, :] = total_of([states[m] * weight[m] for m in range(modes)] + [skip * x])
                return states

            lax.fori_loop(0, steps, step, [start[part] for start in starts], unroll=4)


def final_kernel(modes, *refs):
    low_refs, high_refs = refs[0:2], refs[2:4]
    query_ref, carry_ref, near_ref, far_ref, decay_ref, out_ref, sum_ref, held_ref, out_sem = refs[4:]
    _, groups, tokens, _ = sum_ref.shape
    steps = tokens // SUBS
    core = lax.axis_index("tp") % 2

    def copy_out(group):
        return pltpu.make_async_copy(held_ref.at[group], out_ref.at[pl.ds(group * LANES, LANES)], out_sem.at[group])

    for group in range(groups):
        lanes = pl.ds(group * LANES, LANES)
        decay = [wide(decay_ref, mode, lanes) for mode in range(modes)]
        local_refs = low_refs if group < groups // 2 else high_refs
        for part, start_ref in enumerate((near_ref, far_ref)):
            local_ref = local_refs[part]
            first = [start_ref[mode, :, lanes] * wide(carry_ref, mode, lanes) for mode in range(modes)]

            def step(i, states):
                at = pl.ds(i, SUBS, stride=steps)
                sum_ref[core ^ part, group, at, :] = total_of([local_ref[group % (groups // 2), at, :]] + states)
                return [states[m] * decay[m] for m in range(modes)]

            lax.fori_loop(0, steps, step, first, unroll=8)
        for tile in range(2 * tokens // LANES):
            rows = pl.ds(tile * LANES, LANES)
            mixed = jnp.concatenate([sum_ref[part, group, pl.ds(tile * LANES // 2, LANES // 2), :] for part in range(2)])
            gated = mixed * query_ref[rows, lanes].astype(F32)
            held_ref[group, :, rows] = gated.T.astype(BF16)
        copy_out(group).start()
    for group in range(groups):
        copy_out(group).wait()


def per_device(qkv, residues, spans, skip):
    _, span_tokens, _ = qkv.shape
    devices = lax.axis_size("tp")
    chips = devices // 2
    channels, modes = residues.shape
    tokens = devices * span_tokens
    half = tokens // 2
    groups = channels // LANES
    steps = half // SUBS
    core = lax.axis_index("tp") % 2

    outs = pl.pallas_call(
        open_kernel,
        in_specs=[VMEM],
        out_specs=[VMEM] * (chips + 2),
        out_shape=[jax.ShapeDtypeStruct((2, span_tokens, channels), BF16)] * chips
        + [jax.ShapeDtypeStruct((chips, span_tokens, channels), BF16)] * 2,
        compiler_params=PARAMS,
    )(qkv)
    code, (low, high) = list(outs[:chips]), outs[chips:]
    for k in (1, 3, 2):
        code[k] = across_chips(code[k], k)
    query = jnp.concatenate([low, high])
    query = lax.all_to_all(query, "tp", 0, 0).reshape(tokens, channels)
    near_code = jnp.stack([piece[0] for piece in code])
    far_code = across_core(jnp.stack([piece[1] for piece in code]))

    rates = 1.0 / spans.T
    weight = residues.T * jnp.sqrt(rates) * (1.0 / SCALE)
    decay = jnp.exp(-rates)
    step_decay = jnp.exp(-rates * steps)
    sub_index = jnp.arange(SUBS, dtype=jnp.int32)

    def first_token(side):
        return (2 * span_tokens * (sub_index // 2) + steps * (sub_index % 2) + span_tokens * side).astype(F32)[None, :, None]

    def tail(side):
        return jnp.exp(-rates[:, None, :] * (tokens - steps - first_token(side)))

    def start(side):
        return weight[:, None, :] * jnp.exp(-rates[:, None, :] * (first_token(side) + 1.0))

    def states(code, tail, earlier):
        return pl.pallas_call(
            functools.partial(state_kernel, modes),
            in_specs=[VMEM] * 4,
            out_specs=[VMEM] * 3,
            out_shape=[
                jax.ShapeDtypeStruct((groups, half, LANES), F32),
                jax.ShapeDtypeStruct((modes, SUBS, channels), F32),
                jax.ShapeDtypeStruct((modes, channels), F32),
            ],
            compiler_params=PARAMS,
            cost_estimate=pl.CostEstimate(flops=1000, bytes_accessed=1000, transcendentals=0),
        )(code, decay, tail, earlier)

    near_drive, near_subs, block = states(near_code, tail(core), jnp.zeros((modes, channels), F32))
    far_drive, far_subs, block = states(far_code, tail(1 - core), block)

    local = [
        pl.pallas_call(
            functools.partial(local_kernel, modes, begin),
            in_specs=[VMEM] * 8,
            out_specs=[VMEM] * 2,
            out_shape=[jax.ShapeDtypeStruct((groups // 2, half, LANES), F32)] * 2,
            compiler_params=PARAMS,
            cost_estimate=pl.CostEstimate(flops=40_000_000, bytes_accessed=4_000_000, transcendentals=0),
        )(
            near_drive, far_drive, near_subs, far_subs, decay, step_decay, weight,
            skip.reshape(1, channels) * (1.0 / SCALE),
        )
        for begin in (0, groups // 2)
    ]

    index = lax.axis_index("ctx")
    col, row = index % 4, index // 4

    def power(count):
        count = jnp.asarray(count)
        return jnp.where(count >= 0, jnp.exp(-rates * jnp.maximum(count, 0).astype(F32)), 0.0)

    others = [across_blocks(block, k) for k in (2, 1, 3)]
    others, query, local[0] = lax.optimization_barrier((others, query, local[0]))
    before = jnp.zeros_like(block)
    total = power(tokens * (3 - col)) * block
    for k, other in zip((2, 1, 3), others):
        before = before + power(tokens * (col - 1 - (col ^ k))) * other
        total = total + power(tokens * (3 - (col ^ k))) * other
    others = [across_blocks(total, 4 * k) for k in (2, 1, 3)]
    others, local[1] = lax.optimization_barrier((others, local[1]))
    carry = jnp.zeros_like(block)
    for k, other in zip((2, 1, 3), others):
        carry = carry + power(4 * tokens * (row - 1 - (row ^ k))) * other
    carry = before + power(tokens * col) * carry

    return pl.pallas_call(
        functools.partial(final_kernel, modes),
        in_specs=[VMEM] * 9,
        out_specs=pl.BlockSpec(memory_space=pl.ANY),
        out_shape=jax.ShapeDtypeStruct((channels, tokens), BF16),
        scratch_shapes=[
            pltpu.VMEM((2, groups, half, LANES), F32),
            pltpu.VMEM((groups, LANES, tokens), BF16),
            pltpu.SemaphoreType.DMA((groups,)),
        ],
        compiler_params=PARAMS,
        cost_estimate=pl.CostEstimate(flops=40_000_000, bytes_accessed=2_000_000, transcendentals=0),
    )(*local[0], *local[1], query, carry, start(core), start(1 - core), decay)


def solution(mesh):
    return jax.shard_map(
        per_device,
        mesh=mesh,
        in_specs=(P(None, ("ctx", "tp"), None), P("tp", None), P("tp", None), P("tp")),
        out_specs=P("tp", "ctx"),
        check_vma=False,
    )
```

```python
import functools

import jax
import jax.numpy as jnp
from jax import lax
from jax.experimental import pallas as pl
from jax.experimental.pallas import tpu as pltpu
from jax.sharding import PartitionSpec as P

F32 = jnp.float32
BF16 = jnp.bfloat16
SUBS = 8
LANES = 128
SCALE = 1024.0
CHIP_ORDER = (2, 1, 3)
VMEM = pl.BlockSpec(memory_space=pltpu.VMEM)
PARAMS = pltpu.CompilerParams(vmem_limit_bytes=32 * 1024 * 1024)


def encode(scaled):
    size = jnp.maximum(jnp.abs(scaled), 1.0)
    square = size * size
    return (scaled * (square * square * square * size)).astype(BF16)


def decode(code):
    code = code.astype(F32)
    half = lax.rsqrt(jnp.maximum(jnp.abs(code), 1.0))
    eighth = lax.rsqrt(lax.rsqrt(half))
    return code * (half * eighth * eighth * eighth)


def open_kernel(qkv_ref, *refs):
    *code_refs, low_ref, high_ref = refs
    _, _, width = code_refs[0].shape
    place = lax.axis_index("tp")
    chips = len(code_refs)
    for k, code_ref in enumerate(code_refs):
        for flip in range(2):
            lanes = pl.ds(pl.multiple_of((place ^ (2 * k + flip)) * width, width), width)
            code_ref[flip] = encode(qkv_ref[1, :, lanes].astype(F32) * qkv_ref[2, :, lanes].astype(F32) * SCALE)
    for half, out_ref in enumerate((low_ref, high_ref)):
        for part in range(chips):
            out_ref[part] = qkv_ref[0, :, pl.ds((half * chips + part) * width, width)]


def across_core(value):
    return lax.ppermute(value, "tp", [(i, i ^ 1) for i in range(lax.axis_size("tp"))])


def across_chips(value, k):
    return lax.ppermute(value, "tp", [(i, i ^ 2 * k) for i in range(lax.axis_size("tp"))])


def across_blocks(value, bits):
    return lax.ppermute(value, "ctx", [(i, i ^ bits) for i in range(lax.axis_size("ctx"))])


def wide(ref, mode, lanes):
    return jnp.broadcast_to(ref[mode : mode + 1, lanes], (SUBS, LANES))


def total_of(parts):
    while len(parts) > 1:
        parts = [parts[j] + parts[j + 1] if j + 1 < len(parts) else parts[j] for j in range(0, len(parts), 2)]
    return parts[0]


def state_kernel(modes, code_ref, decay_ref, tail_ref, earlier_ref, drive_ref, sub_ref, block_ref):
    chips, tokens, channels = code_ref.shape
    steps = chips * tokens // SUBS
    chip = lax.axis_index("tp") // 2
    for source in range(chips):
        k = chip ^ source
        slot = k % 2 * 2 + k // 2
        for group in range(channels // LANES):
            lanes = pl.ds(group * LANES, LANES)
            drive_ref[group, pl.ds(source * tokens, tokens), :] = decode(code_ref[slot, :, lanes])
    for group in range(channels // LANES):
        lanes = pl.ds(group * LANES, LANES)
        decay = [wide(decay_ref, mode, lanes) for mode in range(modes)]

        def step(i, states):
            x = drive_ref[group, pl.ds(i, SUBS, stride=steps), :]
            return [states[m] * decay[m] + x for m in range(modes)]

        zero = jnp.zeros((SUBS, LANES), F32)
        states = lax.fori_loop(0, steps, step, [zero] * modes, unroll=8)
        for mode in range(modes):
            sub_ref[mode, :, lanes] = states[mode]
            block_ref[mode : mode + 1, lanes] = earlier_ref[mode : mode + 1, lanes] + jnp.sum(
                states[mode] * tail_ref[mode, :, lanes], axis=0, keepdims=True
            )


def first_states(near, far, decay_32, core):
    row = lax.broadcasted_iota(jnp.int32, (SUBS, LANES), 0)
    odd = row % 2 == 1
    decay_64 = decay_32 * decay_32
    decay_128 = decay_64 * decay_64
    first = jnp.where(core == 0, near, far)
    second = jnp.where(core == 0, far, near)
    first_before, second_before = pltpu.roll(first, 1, 0), pltpu.roll(second, 1, 0)
    first_whole = first + decay_32 * first_before
    held = second + decay_32 * second_before + decay_64 * first_whole
    held = held + decay_128 * jnp.where(row >= 2, pltpu.roll(held, 2, 0), 0.0)
    held = held + decay_128 * decay_128 * jnp.where(row >= 4, pltpu.roll(held, 4, 0), 0.0)
    into = jnp.where(odd, pltpu.roll(held, 2, 0), pltpu.roll(held, 1, 0))
    into = jnp.where(row >= 2, into, 0.0)
    middle = decay_64 * into + jnp.where(odd, first_whole, pltpu.roll(first_whole, SUBS - 1, 0))
    first = jnp.where(odd, decay_32 * into + first_before, into)
    second = jnp.where(odd, decay_32 * middle + second_before, middle)
    return jnp.where(core == 0, first, second), jnp.where(core == 0, second, first)


def local_kernel(modes, begin, *refs):
    drive_refs, (near_ref, far_ref, decay_ref, step_decay_ref, weight_ref, skip_ref), out_refs = refs[:2], refs[2:8], refs[8:]
    groups, tokens, _ = out_refs[0].shape
    steps = tokens // SUBS
    core = lax.axis_index("tp") % 2
    for group in range(groups):
        lanes = pl.ds((begin + group) * LANES, LANES)
        decay = [wide(decay_ref, mode, lanes) for mode in range(modes)]
        weight = [wide(weight_ref, mode, lanes) for mode in range(modes)]
        skip = jnp.broadcast_to(skip_ref[0:1, lanes], (SUBS, LANES))
        starts = [
            first_states(near_ref[m, :, lanes], far_ref[m, :, lanes], wide(step_decay_ref, m, lanes), core)
            for m in range(modes)
        ]
        for part, (drive_ref, out_ref) in enumerate(zip(drive_refs, out_refs)):

            def step(i, states):
                at = pl.ds(i, SUBS, stride=steps)
                x = drive_ref[begin + group, at, :]
                states = [states[m] * decay[m] + x for m in range(modes)]
                out_ref[group, at, :] = total_of([states[m] * weight[m] for m in range(modes)] + [skip * x])
                return states

            lax.fori_loop(0, steps, step, [start[part] for start in starts], unroll=4)


def final_kernel(modes, *refs):
    low_refs, high_refs = refs[0:2], refs[2:4]
    query_ref, carry_ref, near_ref, far_ref, decay_ref, out_ref, sum_ref, held_ref, out_sem = refs[4:]
    _, groups, tokens, _ = sum_ref.shape
    steps = tokens // SUBS
    core = lax.axis_index("tp") % 2

    def copy_out(group):
        return pltpu.make_async_copy(held_ref.at[group], out_ref.at[pl.ds(group * LANES, LANES)], out_sem.at[group])

    for group in range(groups):
        lanes = pl.ds(group * LANES, LANES)
        decay = [wide(decay_ref, mode, lanes) for mode in range(modes)]
        local_refs = low_refs if group < groups // 2 else high_refs
        for part, start_ref in enumerate((near_ref, far_ref)):
            local_ref = local_refs[part]
            first = [start_ref[mode, :, lanes] * wide(carry_ref, mode, lanes) for mode in range(modes)]

            def step(i, states):
                at = pl.ds(i, SUBS, stride=steps)
                sum_ref[core ^ part, group, at, :] = total_of([local_ref[group % (groups // 2), at, :]] + states)
                return [states[m] * decay[m] for m in range(modes)]

            lax.fori_loop(0, steps, step, first, unroll=8)
        for tile in range(2 * tokens // LANES):
            rows = pl.ds(tile * LANES, LANES)
            mixed = jnp.concatenate([sum_ref[part, group, pl.ds(tile * LANES // 2, LANES // 2), :] for part in range(2)])
            gated = mixed * query_ref[rows, lanes].astype(F32)
            held_ref[group, :, rows] = gated.T.astype(BF16)
        copy_out(group).start()
    for group in range(groups):
        copy_out(group).wait()


def per_device(qkv, residues, spans, skip):
    _, span_tokens, _ = qkv.shape
    devices = lax.axis_size("tp")
    chips = devices // 2
    channels, modes = residues.shape
    tokens = devices * span_tokens
    half = tokens // 2
    groups = channels // LANES
    steps = half // SUBS
    core = lax.axis_index("tp") % 2

    outs = pl.pallas_call(
        open_kernel,
        in_specs=[VMEM],
        out_specs=[VMEM] * (chips + 2),
        out_shape=[jax.ShapeDtypeStruct((2, span_tokens, channels), BF16)] * chips
        + [jax.ShapeDtypeStruct((chips, span_tokens, channels), BF16)] * 2,
        compiler_params=PARAMS,
    )(qkv)
    code, (low, high) = list(outs[:chips]), outs[chips:]
    for k in CHIP_ORDER:
        code[k] = across_chips(code[k], k)
    query = jnp.concatenate([low, high])
    query = lax.all_to_all(query, "tp", 0, 0).reshape(tokens, channels)
    code = [code[0]] + [code[k] for k in CHIP_ORDER]
    near_code = jnp.stack([piece[0] for piece in code])
    far_code = across_core(jnp.stack([piece[1] for piece in code]))

    rates = 1.0 / spans.T
    weight = residues.T * jnp.sqrt(rates) * (1.0 / SCALE)
    decay = jnp.exp(-rates)
    step_decay = jnp.exp(-rates * steps)
    sub_index = jnp.arange(SUBS, dtype=jnp.int32)

    def first_token(side):
        return (2 * span_tokens * (sub_index // 2) + steps * (sub_index % 2) + span_tokens * side).astype(F32)[None, :, None]

    def tail(side):
        return jnp.exp(-rates[:, None, :] * (tokens - steps - first_token(side)))

    def start(side):
        return weight[:, None, :] * jnp.exp(-rates[:, None, :] * (first_token(side) + 1.0))

    def states(code, tail, earlier):
        return pl.pallas_call(
            functools.partial(state_kernel, modes),
            in_specs=[VMEM] * 4,
            out_specs=[VMEM] * 3,
            out_shape=[
                jax.ShapeDtypeStruct((groups, half, LANES), F32),
                jax.ShapeDtypeStruct((modes, SUBS, channels), F32),
                jax.ShapeDtypeStruct((modes, channels), F32),
            ],
            compiler_params=PARAMS,
            cost_estimate=pl.CostEstimate(flops=1000, bytes_accessed=1000, transcendentals=0),
        )(code, decay, tail, earlier)

    near_drive, near_subs, block = states(near_code, tail(core), jnp.zeros((modes, channels), F32))
    far_drive, far_subs, block = states(far_code, tail(1 - core), block)

    local = [
        pl.pallas_call(
            functools.partial(local_kernel, modes, begin),
            in_specs=[VMEM] * 8,
            out_specs=[VMEM] * 2,
            out_shape=[jax.ShapeDtypeStruct((groups // 2, half, LANES), F32)] * 2,
            compiler_params=PARAMS,
            cost_estimate=pl.CostEstimate(flops=40_000_000, bytes_accessed=4_000_000, transcendentals=0),
        )(
            near_drive, far_drive, near_subs, far_subs, decay, step_decay, weight,
            skip.reshape(1, channels) * (1.0 / SCALE),
        )
        for begin in (0, groups // 2)
    ]

    index = lax.axis_index("ctx")
    col, row = index % 4, index // 4

    def power(count):
        count = jnp.asarray(count)
        return jnp.where(count >= 0, jnp.exp(-rates * jnp.maximum(count, 0).astype(F32)), 0.0)

    others = [across_blocks(block, k) for k in CHIP_ORDER]
    others, query, local[0] = lax.optimization_barrier((others, query, local[0]))
    before = jnp.zeros_like(block)
    total = power(tokens * (3 - col)) * block
    for k, other in zip(CHIP_ORDER, others):
        before = before + power(tokens * (col - 1 - (col ^ k))) * other
        total = total + power(tokens * (3 - (col ^ k))) * other
    others = [across_blocks(total, 4 * k) for k in CHIP_ORDER]
    others, local[1] = lax.optimization_barrier((others, local[1]))
    carry = jnp.zeros_like(block)
    for k, other in zip(CHIP_ORDER, others):
        carry = carry + power(4 * tokens * (row - 1 - (row ^ k))) * other
    carry = before + power(tokens * col) * carry

    return pl.pallas_call(
        functools.partial(final_kernel, modes),
        in_specs=[VMEM] * 9,
        out_specs=pl.BlockSpec(memory_space=pl.ANY),
        out_shape=jax.ShapeDtypeStruct((channels, tokens), BF16),
        scratch_shapes=[
            pltpu.VMEM((2, groups, half, LANES), F32),
            pltpu.VMEM((groups, LANES, tokens), BF16),
            pltpu.SemaphoreType.DMA((groups,)),
        ],
        compiler_params=PARAMS,
        cost_estimate=pl.CostEstimate(flops=40_000_000, bytes_accessed=2_000_000, transcendentals=0),
    )(*local[0], *local[1], query, carry, start(core), start(1 - core), decay)


def solution(mesh):
    return jax.shard_map(
        per_device,
        mesh=mesh,
        in_specs=(P(None, ("ctx", "tp"), None), P("tp", None), P("tp", None), P("tp")),
        out_specs=P("tp", "ctx"),
        check_vma=False,
    )
```

```python
import functools

import jax
import jax.numpy as jnp
from jax import lax
from jax.experimental import pallas as pl
from jax.experimental.pallas import tpu as pltpu
from jax.sharding import PartitionSpec as P

F32 = jnp.float32
BF16 = jnp.bfloat16
SUBS = 8
LANES = 128
SCALE = 1024.0
CHIP_ORDER = (2, 1, 3)
VMEM = pl.BlockSpec(memory_space=pltpu.VMEM)
PARAMS = pltpu.CompilerParams(vmem_limit_bytes=32 * 1024 * 1024)


def encode(scaled):
    size = jnp.maximum(jnp.abs(scaled), 1.0)
    square = size * size
    return (scaled * (square * square * square * size)).astype(BF16)


def decode(code):
    code = code.astype(F32)
    half = lax.rsqrt(jnp.maximum(jnp.abs(code), 1.0))
    eighth = lax.rsqrt(lax.rsqrt(half))
    return code * (half * eighth * eighth * eighth)


def open_kernel(qkv_ref, *refs):
    *code_refs, low_ref, high_ref = refs
    _, _, width = code_refs[0].shape
    place = lax.axis_index("tp")
    chips = len(code_refs)
    for k, code_ref in enumerate(code_refs):
        for flip in range(2):
            lanes = pl.ds(pl.multiple_of((place ^ (2 * k + flip)) * width, width), width)
            code_ref[flip] = encode(qkv_ref[1, :, lanes].astype(F32) * qkv_ref[2, :, lanes].astype(F32) * SCALE)
    for half, out_ref in enumerate((low_ref, high_ref)):
        for part in range(chips):
            out_ref[part] = qkv_ref[0, :, pl.ds((half * chips + part) * width, width)]


def across_core(value):
    return lax.ppermute(value, "tp", [(i, i ^ 1) for i in range(lax.axis_size("tp"))])


def across_chips(value, k):
    return lax.ppermute(value, "tp", [(i, i ^ 2 * k) for i in range(lax.axis_size("tp"))])


def across_blocks(value, bits):
    return lax.ppermute(value, "ctx", [(i, i ^ bits) for i in range(lax.axis_size("ctx"))])


def wide(ref, mode, lanes):
    return jnp.broadcast_to(ref[mode : mode + 1, lanes], (SUBS, LANES))


def total_of(parts):
    while len(parts) > 1:
        parts = [parts[j] + parts[j + 1] if j + 1 < len(parts) else parts[j] for j in range(0, len(parts), 2)]
    return parts[0]


def state_kernel(modes, code_ref, decay_ref, tail_ref, earlier_ref, drive_ref, sub_ref, block_ref):
    chips, tokens, channels = code_ref.shape
    steps = chips * tokens // SUBS
    chip = lax.axis_index("tp") // 2
    for source in range(chips):
        k = chip ^ source
        slot = k % 2 * 2 + k // 2
        for group in range(channels // LANES):
            lanes = pl.ds(group * LANES, LANES)
            drive = decode(code_ref[slot, :, lanes])
            for sub in range(SUBS * source // chips, SUBS * (source + 1) // chips):
                at = sub * steps - source * tokens
                drive_ref[group, pl.ds(sub, steps, stride=SUBS), :] = drive[at : at + steps]
    for group in range(channels // LANES):
        lanes = pl.ds(group * LANES, LANES)
        decay = [wide(decay_ref, mode, lanes) for mode in range(modes)]

        def step(i, states):
            x = drive_ref[group, pl.ds(pl.multiple_of(i * SUBS, SUBS), SUBS), :]
            return [states[m] * decay[m] + x for m in range(modes)]

        zero = jnp.zeros((SUBS, LANES), F32)
        states = lax.fori_loop(0, steps, step, [zero] * modes, unroll=steps)
        for mode in range(modes):
            sub_ref[mode, :, lanes] = states[mode]
            block_ref[mode : mode + 1, lanes] = earlier_ref[mode : mode + 1, lanes] + jnp.sum(
                states[mode] * tail_ref[mode, :, lanes], axis=0, keepdims=True
            )


def first_states(near, far, decay_32, core):
    row = lax.broadcasted_iota(jnp.int32, (SUBS, LANES), 0)
    odd = row % 2 == 1
    decay_64 = decay_32 * decay_32
    decay_128 = decay_64 * decay_64
    first = jnp.where(core == 0, near, far)
    second = jnp.where(core == 0, far, near)
    first_before, second_before = pltpu.roll(first, 1, 0), pltpu.roll(second, 1, 0)
    first_whole = first + decay_32 * first_before
    held = second + decay_32 * second_before + decay_64 * first_whole
    held = held + decay_128 * jnp.where(row >= 2, pltpu.roll(held, 2, 0), 0.0)
    held = held + decay_128 * decay_128 * jnp.where(row >= 4, pltpu.roll(held, 4, 0), 0.0)
    into = jnp.where(odd, pltpu.roll(held, 2, 0), pltpu.roll(held, 1, 0))
    into = jnp.where(row >= 2, into, 0.0)
    middle = decay_64 * into + jnp.where(odd, first_whole, pltpu.roll(first_whole, SUBS - 1, 0))
    first = jnp.where(odd, decay_32 * into + first_before, into)
    second = jnp.where(odd, decay_32 * middle + second_before, middle)
    return jnp.where(core == 0, first, second), jnp.where(core == 0, second, first)


def local_kernel(modes, begin, *refs):
    drive_refs, (near_ref, far_ref, decay_ref, step_decay_ref, weight_ref, skip_ref), out_refs = refs[:2], refs[2:8], refs[8:]
    groups, tokens, _ = out_refs[0].shape
    steps = tokens // SUBS
    core = lax.axis_index("tp") % 2
    for group in range(groups):
        lanes = pl.ds((begin + group) * LANES, LANES)
        decay = [wide(decay_ref, mode, lanes) for mode in range(modes)]
        weight = [wide(weight_ref, mode, lanes) for mode in range(modes)]
        skip = jnp.broadcast_to(skip_ref[0:1, lanes], (SUBS, LANES))
        starts = [
            first_states(near_ref[m, :, lanes], far_ref[m, :, lanes], wide(step_decay_ref, m, lanes), core)
            for m in range(modes)
        ]
        for part, (drive_ref, out_ref) in enumerate(zip(drive_refs, out_refs)):

            def step(i, states):
                at = pl.ds(pl.multiple_of(i * SUBS, SUBS), SUBS)
                x = drive_ref[begin + group, at, :]
                states = [states[m] * decay[m] + x for m in range(modes)]
                out_ref[group, at, :] = total_of([states[m] * weight[m] for m in range(modes)] + [skip * x])
                return states

            lax.fori_loop(0, steps, step, [start[part] for start in starts], unroll=8)


def final_kernel(modes, *refs):
    low_refs, high_refs = refs[0:2], refs[2:4]
    query_ref, carry_ref, near_ref, far_ref, decay_ref, out_ref, sum_ref, held_ref, out_sem = refs[4:]
    _, groups, tokens, _ = sum_ref.shape
    steps = tokens // SUBS
    core = lax.axis_index("tp") % 2

    def copy_out(group):
        return pltpu.make_async_copy(held_ref.at[group], out_ref.at[pl.ds(group * LANES, LANES)], out_sem.at[group])

    for group in range(groups):
        lanes = pl.ds(group * LANES, LANES)
        decay = [wide(decay_ref, mode, lanes) for mode in range(modes)]
        local_refs = low_refs if group < groups // 2 else high_refs
        for part, start_ref in enumerate((near_ref, far_ref)):
            local_ref = local_refs[part]
            first = [start_ref[mode, :, lanes] * wide(carry_ref, mode, lanes) for mode in range(modes)]

            def step(i, states):
                at = pl.ds(pl.multiple_of(i * SUBS, SUBS), SUBS)
                sum_ref[core ^ part, group, at, :] = total_of([local_ref[group % (groups // 2), at, :]] + states)
                return [states[m] * decay[m] for m in range(modes)]

            lax.fori_loop(0, steps, step, first, unroll=steps)
        for tile in range(2 * tokens // LANES):
            rows = pl.ds(tile * LANES, LANES)
            subs = [sum_ref[part, group, pl.ds(2 * tile + j, steps, stride=SUBS), :] for part in range(2) for j in range(2)]
            mixed = jnp.concatenate(subs)
            gated = mixed * query_ref[rows, lanes].astype(F32)
            held_ref[group, :, rows] = gated.T.astype(BF16)
        copy_out(group).start()
    for group in range(groups):
        copy_out(group).wait()


def per_device(qkv, residues, spans, skip):
    _, span_tokens, _ = qkv.shape
    devices = lax.axis_size("tp")
    chips = devices // 2
    channels, modes = residues.shape
    tokens = devices * span_tokens
    half = tokens // 2
    groups = channels // LANES
    steps = half // SUBS
    core = lax.axis_index("tp") % 2

    outs = pl.pallas_call(
        open_kernel,
        in_specs=[VMEM],
        out_specs=[VMEM] * (chips + 2),
        out_shape=[jax.ShapeDtypeStruct((2, span_tokens, channels), BF16)] * chips
        + [jax.ShapeDtypeStruct((chips, span_tokens, channels), BF16)] * 2,
        compiler_params=PARAMS,
    )(qkv)
    code, (low, high) = list(outs[:chips]), outs[chips:]
    for k in CHIP_ORDER:
        code[k] = across_chips(code[k], k)
    query = jnp.concatenate([low, high])
    query = lax.all_to_all(query, "tp", 0, 0).reshape(tokens, channels)
    code = [code[0]] + [code[k] for k in CHIP_ORDER]
    near_code = jnp.stack([piece[0] for piece in code])
    far_code = across_core(jnp.stack([piece[1] for piece in code]))

    rates = 1.0 / spans.T
    weight = residues.T * jnp.sqrt(rates) * (1.0 / SCALE)
    decay = jnp.exp(-rates)
    step_decay = jnp.exp(-rates * steps)
    sub_index = jnp.arange(SUBS, dtype=jnp.int32)

    def first_token(side):
        return (2 * span_tokens * (sub_index // 2) + steps * (sub_index % 2) + span_tokens * side).astype(F32)[None, :, None]

    def tail(side):
        return jnp.exp(-rates[:, None, :] * (tokens - steps - first_token(side)))

    def start(side):
        return weight[:, None, :] * jnp.exp(-rates[:, None, :] * (first_token(side) + 1.0))

    def states(code, tail, earlier):
        return pl.pallas_call(
            functools.partial(state_kernel, modes),
            in_specs=[VMEM] * 4,
            out_specs=[VMEM] * 3,
            out_shape=[
                jax.ShapeDtypeStruct((groups, half, LANES), F32),
                jax.ShapeDtypeStruct((modes, SUBS, channels), F32),
                jax.ShapeDtypeStruct((modes, channels), F32),
            ],
            compiler_params=PARAMS,
            cost_estimate=pl.CostEstimate(flops=1000, bytes_accessed=1000, transcendentals=0),
        )(code, decay, tail, earlier)

    near_drive, near_subs, block = states(near_code, tail(core), jnp.zeros((modes, channels), F32))
    far_drive, far_subs, block = states(far_code, tail(1 - core), block)

    local = [
        pl.pallas_call(
            functools.partial(local_kernel, modes, begin),
            in_specs=[VMEM] * 8,
            out_specs=[VMEM] * 2,
            out_shape=[jax.ShapeDtypeStruct((groups // 2, half, LANES), F32)] * 2,
            compiler_params=PARAMS,
            cost_estimate=pl.CostEstimate(flops=40_000_000, bytes_accessed=4_000_000, transcendentals=0),
        )(
            near_drive, far_drive, near_subs, far_subs, decay, step_decay, weight,
            skip.reshape(1, channels) * (1.0 / SCALE),
        )
        for begin in (0, groups // 2)
    ]

    index = lax.axis_index("ctx")
    col, row = index % 4, index // 4

    def power(count):
        count = jnp.asarray(count)
        return jnp.where(count >= 0, jnp.exp(-rates * jnp.maximum(count, 0).astype(F32)), 0.0)

    others = [across_blocks(block, k) for k in CHIP_ORDER]
    others, query, local[0] = lax.optimization_barrier((others, query, local[0]))
    before = jnp.zeros_like(block)
    total = power(tokens * (3 - col)) * block
    for k, other in zip(CHIP_ORDER, others):
        before = before + power(tokens * (col - 1 - (col ^ k))) * other
        total = total + power(tokens * (3 - (col ^ k))) * other
    others = [across_blocks(total, 4 * k) for k in CHIP_ORDER]
    others, local[1] = lax.optimization_barrier((others, local[1]))
    carry = jnp.zeros_like(block)
    for k, other in zip(CHIP_ORDER, others):
        carry = carry + power(4 * tokens * (row - 1 - (row ^ k))) * other
    carry = before + power(tokens * col) * carry

    return pl.pallas_call(
        functools.partial(final_kernel, modes),
        in_specs=[VMEM] * 9,
        out_specs=pl.BlockSpec(memory_space=pl.ANY),
        out_shape=jax.ShapeDtypeStruct((channels, tokens), BF16),
        scratch_shapes=[
            pltpu.VMEM((2, groups, half, LANES), F32),
            pltpu.VMEM((groups, LANES, tokens), BF16),
            pltpu.SemaphoreType.DMA((groups,)),
        ],
        compiler_params=PARAMS,
        cost_estimate=pl.CostEstimate(flops=40_000_000, bytes_accessed=2_000_000, transcendentals=0),
    )(*local[0], *local[1], query, carry, start(core), start(1 - core), decay)


def solution(mesh):
    return jax.shard_map(
        per_device,
        mesh=mesh,
        in_specs=(P(None, ("ctx", "tp"), None), P("tp", None), P("tp", None), P("tp")),
        out_specs=P("tp", "ctx"),
        check_vma=False,
    )
```

```python
import functools

import jax
import jax.numpy as jnp
from jax import lax
from jax.experimental import pallas as pl
from jax.experimental.pallas import tpu as pltpu
from jax.sharding import PartitionSpec as P

F32 = jnp.float32
BF16 = jnp.bfloat16
SUBS = 8
LANES = 128
SCALE = 1024.0
OPEN_VMEM = 52 * 1024 * 1024
CHIP_ORDER = (2, 1, 3)
VMEM = pl.BlockSpec(memory_space=pltpu.VMEM)
PARAMS = pltpu.CompilerParams(vmem_limit_bytes=32 * 1024 * 1024)


def encode(scaled):
    size = jnp.maximum(jnp.abs(scaled), 1.0)
    square = size * size
    return (scaled * (square * square * square * size)).astype(BF16)


def decode(code):
    code = code.astype(F32)
    half = lax.rsqrt(jnp.maximum(jnp.abs(code), 1.0))
    eighth = lax.rsqrt(lax.rsqrt(half))
    return code * (half * eighth * eighth * eighth)


def open_kernel(qkv_ref, *refs):
    *code_refs, held_ref, held_sem = refs
    _, _, width = code_refs[0].shape
    place = lax.axis_index("tp")

    def fetch(k):
        lanes = pl.ds(pl.multiple_of((place // 2 ^ k) * 2 * width, 2 * width), 2 * width)
        return pltpu.make_async_copy(qkv_ref.at[pl.ds(1, 2), :, lanes], held_ref.at[k], held_sem.at[k])

    order = CHIP_ORDER + (0,)
    for k in order:
        fetch(k).start()
    for k in order:
        fetch(k).wait()
        for flip in range(2):
            half = pl.ds(pl.multiple_of((place % 2 ^ flip) * width, width), width)
            scaled = held_ref[k, 0, :, half].astype(F32) * held_ref[k, 1, :, half].astype(F32) * SCALE
            code_refs[k][flip] = encode(scaled)


def query_kernel(qkv_ref, query_ref, moved_ref, sem):
    parts, _, width = moved_ref.shape
    copies = [pltpu.make_async_copy(moved_ref.at[part], query_ref.at[part], sem.at[part]) for part in range(parts)]
    for part in range(parts):
        moved_ref[part] = qkv_ref[0, :, pl.ds(part * width, width)]
        copies[part].start()
    for copy in copies:
        copy.wait()


def across_core(value):
    return lax.ppermute(value, "tp", [(i, i ^ 1) for i in range(lax.axis_size("tp"))])


def across_chips(value, k):
    return lax.ppermute(value, "tp", [(i, i ^ 2 * k) for i in range(lax.axis_size("tp"))])


def across_blocks(value, bits):
    return lax.ppermute(value, "ctx", [(i, i ^ bits) for i in range(lax.axis_size("ctx"))])


def wide(ref, mode, lanes):
    return jnp.broadcast_to(ref[mode : mode + 1, lanes], (SUBS, LANES))


def total_of(parts):
    while len(parts) > 1:
        parts = [parts[j] + parts[j + 1] if j + 1 < len(parts) else parts[j] for j in range(0, len(parts), 2)]
    return parts[0]


def state_kernel(modes, code_ref, decay_ref, tail_ref, earlier_ref, drive_ref, sub_ref, block_ref):
    chips, tokens, channels = code_ref.shape
    steps = chips * tokens // SUBS
    chip = lax.axis_index("tp") // 2
    for source in range(chips):
        k = chip ^ source
        slot = k % 2 * 2 + k // 2
        for group in range(channels // LANES):
            lanes = pl.ds(group * LANES, LANES)
            drive = decode(code_ref[slot, :, lanes])
            for sub in range(SUBS * source // chips, SUBS * (source + 1) // chips):
                at = sub * steps - source * tokens
                drive_ref[group, pl.ds(sub, steps, stride=SUBS), :] = drive[at : at + steps]
    for group in range(channels // LANES):
        lanes = pl.ds(group * LANES, LANES)
        decay = [wide(decay_ref, mode, lanes) for mode in range(modes)]

        def step(i, states):
            x = drive_ref[group, pl.ds(pl.multiple_of(i * SUBS, SUBS), SUBS), :]
            return [states[m] * decay[m] + x for m in range(modes)]

        zero = jnp.zeros((SUBS, LANES), F32)
        states = lax.fori_loop(0, steps, step, [zero] * modes, unroll=steps)
        for mode in range(modes):
            sub_ref[mode, :, lanes] = states[mode]
            block_ref[mode : mode + 1, lanes] = earlier_ref[mode : mode + 1, lanes] + jnp.sum(
                states[mode] * tail_ref[mode, :, lanes], axis=0, keepdims=True
            )


def first_states(near, far, decay_32, core):
    row = lax.broadcasted_iota(jnp.int32, (SUBS, LANES), 0)
    odd = row % 2 == 1
    decay_64 = decay_32 * decay_32
    decay_128 = decay_64 * decay_64
    first = jnp.where(core == 0, near, far)
    second = jnp.where(core == 0, far, near)
    first_before, second_before = pltpu.roll(first, 1, 0), pltpu.roll(second, 1, 0)
    first_whole = first + decay_32 * first_before
    held = second + decay_32 * second_before + decay_64 * first_whole
    held = held + decay_128 * jnp.where(row >= 2, pltpu.roll(held, 2, 0), 0.0)
    held = held + decay_128 * decay_128 * jnp.where(row >= 4, pltpu.roll(held, 4, 0), 0.0)
    into = jnp.where(odd, pltpu.roll(held, 2, 0), pltpu.roll(held, 1, 0))
    into = jnp.where(row >= 2, into, 0.0)
    middle = decay_64 * into + jnp.where(odd, first_whole, pltpu.roll(first_whole, SUBS - 1, 0))
    first = jnp.where(odd, decay_32 * into + first_before, into)
    second = jnp.where(odd, decay_32 * middle + second_before, middle)
    return jnp.where(core == 0, first, second), jnp.where(core == 0, second, first)


def local_kernel(modes, begin, *refs):
    drive_refs, (near_ref, far_ref, decay_ref, step_decay_ref, weight_ref, skip_ref), out_refs = refs[:2], refs[2:8], refs[8:]
    groups, tokens, _ = out_refs[0].shape
    steps = tokens // SUBS
    core = lax.axis_index("tp") % 2
    for group in range(groups):
        lanes = pl.ds((begin + group) * LANES, LANES)
        decay = [wide(decay_ref, mode, lanes) for mode in range(modes)]
        weight = [wide(weight_ref, mode, lanes) for mode in range(modes)]
        skip = jnp.broadcast_to(skip_ref[0:1, lanes], (SUBS, LANES))
        starts = [
            first_states(near_ref[m, :, lanes], far_ref[m, :, lanes], wide(step_decay_ref, m, lanes), core)
            for m in range(modes)
        ]
        for part, (drive_ref, out_ref) in enumerate(zip(drive_refs, out_refs)):

            def step(i, states):
                at = pl.ds(pl.multiple_of(i * SUBS, SUBS), SUBS)
                x = drive_ref[begin + group, at, :]
                states = [states[m] * decay[m] + x for m in range(modes)]
                out_ref[group, at, :] = total_of([states[m] * weight[m] for m in range(modes)] + [skip * x])
                return states

            lax.fori_loop(0, steps, step, [start[part] for start in starts], unroll=8)


def final_kernel(modes, *refs):
    low_refs, high_refs = refs[0:2], refs[2:4]
    query_ref, carry_ref, near_ref, far_ref, decay_ref, out_ref, sum_ref, held_ref, out_sem = refs[4:]
    _, groups, tokens, _ = sum_ref.shape
    steps = tokens // SUBS
    core = lax.axis_index("tp") % 2

    def copy_out(group):
        return pltpu.make_async_copy(held_ref.at[group], out_ref.at[pl.ds(group * LANES, LANES)], out_sem.at[group])

    for group in range(groups):
        lanes = pl.ds(group * LANES, LANES)
        decay = [wide(decay_ref, mode, lanes) for mode in range(modes)]
        local_refs = low_refs if group < groups // 2 else high_refs
        for part, start_ref in enumerate((near_ref, far_ref)):
            local_ref = local_refs[part]
            first = [start_ref[mode, :, lanes] * wide(carry_ref, mode, lanes) for mode in range(modes)]

            def step(i, states):
                at = pl.ds(pl.multiple_of(i * SUBS, SUBS), SUBS)
                sum_ref[core ^ part, group, at, :] = total_of([local_ref[group % (groups // 2), at, :]] + states)
                return [states[m] * decay[m] for m in range(modes)]

            lax.fori_loop(0, steps, step, first, unroll=steps)
        for tile in range(2 * tokens // LANES):
            rows = pl.ds(tile * LANES, LANES)
            subs = [sum_ref[part, group, pl.ds(2 * tile + j, steps, stride=SUBS), :] for part in range(2) for j in range(2)]
            mixed = jnp.concatenate(subs)
            gated = mixed * query_ref[rows, lanes].astype(F32)
            held_ref[group, :, rows] = gated.T.astype(BF16)
        copy_out(group).start()
    for group in range(groups):
        copy_out(group).wait()


def per_device(qkv, residues, spans, skip):
    _, span_tokens, _ = qkv.shape
    devices = lax.axis_size("tp")
    chips = devices // 2
    channels, modes = residues.shape
    tokens = devices * span_tokens
    half = tokens // 2
    groups = channels // LANES
    steps = half // SUBS
    core = lax.axis_index("tp") % 2

    code = list(
        pl.pallas_call(
            open_kernel,
            in_specs=[pl.BlockSpec(memory_space=pl.ANY)],
            out_specs=[VMEM] * chips,
            out_shape=[jax.ShapeDtypeStruct((2, span_tokens, channels), BF16)] * chips,
            scratch_shapes=[
                pltpu.VMEM((chips, 2, span_tokens, 2 * channels), BF16),
                pltpu.SemaphoreType.DMA((chips,)),
            ],
            compiler_params=pltpu.CompilerParams(vmem_limit_bytes=OPEN_VMEM),
        )(qkv)
    )
    query = pl.pallas_call(
        query_kernel,
        in_specs=[VMEM],
        out_specs=pl.BlockSpec(memory_space=pl.ANY),
        out_shape=jax.ShapeDtypeStruct((devices, span_tokens, channels), BF16),
        scratch_shapes=[pltpu.VMEM((devices, span_tokens, channels), BF16), pltpu.SemaphoreType.DMA((devices,))],
        compiler_params=PARAMS,
    )(qkv)
    for k in CHIP_ORDER:
        code[k] = across_chips(code[k], k)
    query = lax.all_to_all(query, "tp", 0, 0).reshape(tokens, channels)
    code = [code[0]] + [code[k] for k in CHIP_ORDER]
    near_code = jnp.stack([piece[0] for piece in code])
    far_code = across_core(jnp.stack([piece[1] for piece in code]))

    rates = 1.0 / spans.T
    weight = residues.T * jnp.sqrt(rates) * (1.0 / SCALE)
    decay = jnp.exp(-rates)
    sub_index = jnp.arange(SUBS, dtype=jnp.int32)

    def first_token(side):
        return (2 * span_tokens * (sub_index // 2) + steps * (sub_index % 2) + span_tokens * side).astype(F32)[None, :, None]

    def tail(side):
        return jnp.exp(-rates[:, None, :] * (tokens - steps - first_token(side)))

    def start(side):
        return weight[:, None, :] * jnp.exp(-rates[:, None, :] * (first_token(side) + 1.0))

    def states(code, tail, earlier):
        return pl.pallas_call(
            functools.partial(state_kernel, modes),
            in_specs=[VMEM] * 4,
            out_specs=[VMEM] * 3,
            out_shape=[
                jax.ShapeDtypeStruct((groups, half, LANES), F32),
                jax.ShapeDtypeStruct((modes, SUBS, channels), F32),
                jax.ShapeDtypeStruct((modes, channels), F32),
            ],
            compiler_params=PARAMS,
            cost_estimate=pl.CostEstimate(flops=1000, bytes_accessed=1000, transcendentals=0),
        )(code, decay, tail, earlier)

    near_drive, near_subs, block = states(near_code, tail(core), jnp.zeros((modes, channels), F32))
    far_drive, far_subs, block = states(far_code, tail(1 - core), block)
    rates, weight, block = lax.optimization_barrier((rates, weight, block))
    step_decay = jnp.exp(-rates * steps)

    local = [
        pl.pallas_call(
            functools.partial(local_kernel, modes, begin),
            in_specs=[VMEM] * 8,
            out_specs=[VMEM] * 2,
            out_shape=[jax.ShapeDtypeStruct((groups // 2, half, LANES), F32)] * 2,
            compiler_params=PARAMS,
            cost_estimate=pl.CostEstimate(flops=40_000_000, bytes_accessed=4_000_000, transcendentals=0),
        )(
            near_drive, far_drive, near_subs, far_subs, decay, step_decay, weight,
            skip.reshape(1, channels) * (1.0 / SCALE),
        )
        for begin in (0, groups // 2)
    ]

    index = lax.axis_index("ctx")
    col, row = index % 4, index // 4

    def power(count):
        count = jnp.asarray(count)
        return jnp.where(count >= 0, jnp.exp(-rates * jnp.maximum(count, 0).astype(F32)), 0.0)

    others = [across_blocks(block, k) for k in CHIP_ORDER]
    others, query, local[0] = lax.optimization_barrier((others, query, local[0]))
    before = jnp.zeros_like(block)
    total = power(tokens * (3 - col)) * block
    for k, other in zip(CHIP_ORDER, others):
        before = before + power(tokens * (col - 1 - (col ^ k))) * other
        total = total + power(tokens * (3 - (col ^ k))) * other
    others = [across_blocks(total, 4 * k) for k in CHIP_ORDER]
    others, local[1] = lax.optimization_barrier((others, local[1]))
    carry = jnp.zeros_like(block)
    for k, other in zip(CHIP_ORDER, others):
        carry = carry + power(4 * tokens * (row - 1 - (row ^ k))) * other
    carry = before + power(tokens * col) * carry

    return pl.pallas_call(
        functools.partial(final_kernel, modes),
        in_specs=[VMEM] * 9,
        out_specs=pl.BlockSpec(memory_space=pl.ANY),
        out_shape=jax.ShapeDtypeStruct((channels, tokens), BF16),
        scratch_shapes=[
            pltpu.VMEM((2, groups, half, LANES), F32),
            pltpu.VMEM((groups, LANES, tokens), BF16),
            pltpu.SemaphoreType.DMA((groups,)),
        ],
        compiler_params=PARAMS,
        cost_estimate=pl.CostEstimate(flops=40_000_000, bytes_accessed=2_000_000, transcendentals=0),
    )(*local[0], *local[1], query, carry, start(core), start(1 - core), decay)


def solution(mesh):
    return jax.shard_map(
        per_device,
        mesh=mesh,
        in_specs=(P(None, ("ctx", "tp"), None), P("tp", None), P("tp", None), P("tp")),
        out_specs=P("tp", "ctx"),
        check_vma=False,
    )
```

```python
import functools

import jax
import jax.numpy as jnp
from jax import lax
from jax.experimental import pallas as pl
from jax.experimental.pallas import tpu as pltpu
from jax.sharding import PartitionSpec as P

F32 = jnp.float32
BF16 = jnp.bfloat16
SUBS = 8
LANES = 128
SCALE = 1024.0
OPEN_VMEM = 52 * 1024 * 1024
CHIP_ORDER = (2, 1, 3)
VMEM = pl.BlockSpec(memory_space=pltpu.VMEM)
PARAMS = pltpu.CompilerParams(vmem_limit_bytes=32 * 1024 * 1024)


def encode(scaled):
    size = jnp.maximum(jnp.abs(scaled), 1.0)
    square = size * size
    return (scaled * (square * square * square * size)).astype(BF16)


def decode(code):
    code = code.astype(F32)
    half = lax.rsqrt(jnp.maximum(jnp.abs(code), 1.0))
    eighth = lax.rsqrt(lax.rsqrt(half))
    return code * (half * eighth * eighth * eighth)


def open_kernel(qkv_ref, *refs):
    *code_refs, held_ref, held_sem = refs
    _, _, width = code_refs[0].shape
    place = lax.axis_index("tp")

    def fetch(k):
        lanes = pl.ds(pl.multiple_of((place // 2 ^ k) * 2 * width, 2 * width), 2 * width)
        return pltpu.make_async_copy(qkv_ref.at[pl.ds(1, 2), :, lanes], held_ref.at[k], held_sem.at[k])

    order = CHIP_ORDER + (0,)
    for k in order:
        fetch(k).start()
    for k in order:
        fetch(k).wait()
        for flip in range(2):
            half = pl.ds(pl.multiple_of((place % 2 ^ flip) * width, width), width)
            scaled = held_ref[k, 0, :, half].astype(F32) * held_ref[k, 1, :, half].astype(F32) * SCALE
            code_refs[k][flip] = encode(scaled)


def query_kernel(qkv_ref, query_ref, moved_ref, sem):
    parts, _, width = moved_ref.shape
    copies = [pltpu.make_async_copy(moved_ref.at[part], query_ref.at[part], sem.at[part]) for part in range(parts)]
    for part in range(parts):
        moved_ref[part] = qkv_ref[0, :, pl.ds(part * width, width)]
        copies[part].start()
    for copy in copies:
        copy.wait()


def across_core(value):
    return lax.ppermute(value, "tp", [(i, i ^ 1) for i in range(lax.axis_size("tp"))])


def across_chips(value, k):
    return lax.ppermute(value, "tp", [(i, i ^ 2 * k) for i in range(lax.axis_size("tp"))])


def across_blocks(value, bits):
    return lax.ppermute(value, "ctx", [(i, i ^ bits) for i in range(lax.axis_size("ctx"))])


def wide(ref, mode, lanes):
    return jnp.broadcast_to(ref[mode : mode + 1, lanes], (SUBS, LANES))


def total_of(parts):
    while len(parts) > 1:
        parts = [parts[j] + parts[j + 1] if j + 1 < len(parts) else parts[j] for j in range(0, len(parts), 2)]
    return parts[0]


def state_kernel(modes, code_ref, decay_ref, tail_ref, earlier_ref, drive_ref, sub_ref, block_ref):
    chips, tokens, channels = code_ref.shape
    steps = chips * tokens // SUBS
    chip = lax.axis_index("tp") // 2
    for source in range(chips):
        k = chip ^ source
        slot = k % 2 * 2 + k // 2
        for group in range(channels // LANES):
            lanes = pl.ds(group * LANES, LANES)
            drive = decode(code_ref[slot, :, lanes])
            for sub in range(SUBS * source // chips, SUBS * (source + 1) // chips):
                at = sub * steps - source * tokens
                drive_ref[group, pl.ds(sub, steps, stride=SUBS), :] = drive[at : at + steps]
    for group in range(channels // LANES):
        lanes = pl.ds(group * LANES, LANES)
        decay = [wide(decay_ref, mode, lanes) for mode in range(modes)]

        def step(i, states):
            x = drive_ref[group, pl.ds(pl.multiple_of(i * SUBS, SUBS), SUBS), :]
            return [states[m] * decay[m] + x for m in range(modes)]

        zero = jnp.zeros((SUBS, LANES), F32)
        states = lax.fori_loop(0, steps, step, [zero] * modes, unroll=steps)
        for mode in range(modes):
            sub_ref[mode, :, lanes] = states[mode]
            block_ref[mode : mode + 1, lanes] = earlier_ref[mode : mode + 1, lanes] + jnp.sum(
                states[mode] * tail_ref[mode, :, lanes], axis=0, keepdims=True
            )


def first_states(near, far, decay_32, core):
    row = lax.broadcasted_iota(jnp.int32, (SUBS, LANES), 0)
    odd = row % 2 == 1
    decay_64 = decay_32 * decay_32
    decay_128 = decay_64 * decay_64
    first = jnp.where(core == 0, near, far)
    second = jnp.where(core == 0, far, near)
    first_before, second_before = pltpu.roll(first, 1, 0), pltpu.roll(second, 1, 0)
    first_whole = first + decay_32 * first_before
    held = second + decay_32 * second_before + decay_64 * first_whole
    held = held + decay_128 * jnp.where(row >= 2, pltpu.roll(held, 2, 0), 0.0)
    held = held + decay_128 * decay_128 * jnp.where(row >= 4, pltpu.roll(held, 4, 0), 0.0)
    into = jnp.where(odd, pltpu.roll(held, 2, 0), pltpu.roll(held, 1, 0))
    into = jnp.where(row >= 2, into, 0.0)
    middle = decay_64 * into + jnp.where(odd, first_whole, pltpu.roll(first_whole, SUBS - 1, 0))
    first = jnp.where(odd, decay_32 * into + first_before, into)
    second = jnp.where(odd, decay_32 * middle + second_before, middle)
    return jnp.where(core == 0, first, second), jnp.where(core == 0, second, first)


def local_kernel(modes, begin, *refs):
    drive_refs, (near_ref, far_ref, decay_ref, step_decay_ref, weight_ref, skip_ref), out_refs = refs[:2], refs[2:8], refs[8:]
    groups, tokens, _ = out_refs[0].shape
    steps = tokens // SUBS
    core = lax.axis_index("tp") % 2
    for group in range(groups):
        lanes = pl.ds((begin + group) * LANES, LANES)
        decay = [wide(decay_ref, mode, lanes) for mode in range(modes)]
        weight = [wide(weight_ref, mode, lanes) for mode in range(modes)]
        skip = jnp.broadcast_to(skip_ref[0:1, lanes], (SUBS, LANES))
        starts = [
            first_states(near_ref[m, :, lanes], far_ref[m, :, lanes], wide(step_decay_ref, m, lanes), core)
            for m in range(modes)
        ]
        for part, (drive_ref, out_ref) in enumerate(zip(drive_refs, out_refs)):

            def step(i, states):
                at = pl.ds(pl.multiple_of(i * SUBS, SUBS), SUBS)
                x = drive_ref[begin + group, at, :]
                states = [states[m] * decay[m] + x for m in range(modes)]
                out_ref[group, at, :] = total_of([states[m] * weight[m] for m in range(modes)] + [skip * x])
                return states

            lax.fori_loop(0, steps, step, [start[part] for start in starts], unroll=8)


def final_kernel(modes, early, *refs):
    row = lax.axis_index("ctx") // 4

    @pl.when(row == 0 if early else row > 0)
    def _():
        finish(modes, *refs[: 9], *refs[9 if early else 10 :])


def finish(modes, *refs):
    low_refs, high_refs = refs[0:2], refs[2:4]
    query_ref, carry_ref, near_ref, far_ref, decay_ref, out_ref, sum_ref, held_ref, out_sem = refs[4:]
    _, groups, tokens, _ = sum_ref.shape
    steps = tokens // SUBS
    core = lax.axis_index("tp") % 2

    def copy_out(group):
        return pltpu.make_async_copy(held_ref.at[group], out_ref.at[pl.ds(group * LANES, LANES)], out_sem.at[group])

    for group in range(groups):
        lanes = pl.ds(group * LANES, LANES)
        decay = [wide(decay_ref, mode, lanes) for mode in range(modes)]
        local_refs = low_refs if group < groups // 2 else high_refs
        for part, start_ref in enumerate((near_ref, far_ref)):
            local_ref = local_refs[part]
            first = [start_ref[mode, :, lanes] * wide(carry_ref, mode, lanes) for mode in range(modes)]

            def step(i, states):
                at = pl.ds(pl.multiple_of(i * SUBS, SUBS), SUBS)
                sum_ref[core ^ part, group, at, :] = total_of([local_ref[group % (groups // 2), at, :]] + states)
                return [states[m] * decay[m] for m in range(modes)]

            lax.fori_loop(0, steps, step, first, unroll=steps)
        for tile in range(2 * tokens // LANES):
            rows = pl.ds(tile * LANES, LANES)
            subs = [sum_ref[part, group, pl.ds(2 * tile + j, steps, stride=SUBS), :] for part in range(2) for j in range(2)]
            mixed = jnp.concatenate(subs)
            gated = mixed * query_ref[rows, lanes].astype(F32)
            held_ref[group, :, rows] = gated.T.astype(BF16)
        copy_out(group).start()
    for group in range(groups):
        copy_out(group).wait()


def per_device(qkv, residues, spans, skip):
    _, span_tokens, _ = qkv.shape
    devices = lax.axis_size("tp")
    chips = devices // 2
    channels, modes = residues.shape
    tokens = devices * span_tokens
    half = tokens // 2
    groups = channels // LANES
    steps = half // SUBS
    core = lax.axis_index("tp") % 2

    code = list(
        pl.pallas_call(
            open_kernel,
            in_specs=[pl.BlockSpec(memory_space=pl.ANY)],
            out_specs=[VMEM] * chips,
            out_shape=[jax.ShapeDtypeStruct((2, span_tokens, channels), BF16)] * chips,
            scratch_shapes=[
                pltpu.VMEM((chips, 2, span_tokens, 2 * channels), BF16),
                pltpu.SemaphoreType.DMA((chips,)),
            ],
            compiler_params=pltpu.CompilerParams(vmem_limit_bytes=OPEN_VMEM),
        )(qkv)
    )
    query = pl.pallas_call(
        query_kernel,
        in_specs=[VMEM],
        out_specs=pl.BlockSpec(memory_space=pl.ANY),
        out_shape=jax.ShapeDtypeStruct((devices, span_tokens, channels), BF16),
        scratch_shapes=[pltpu.VMEM((devices, span_tokens, channels), BF16), pltpu.SemaphoreType.DMA((devices,))],
        compiler_params=PARAMS,
    )(qkv)
    for k in CHIP_ORDER:
        code[k] = across_chips(code[k], k)
    query = lax.all_to_all(query, "tp", 0, 0).reshape(tokens, channels)
    code = [code[0]] + [code[k] for k in CHIP_ORDER]
    near_code = jnp.stack([piece[0] for piece in code])
    far_code = across_core(jnp.stack([piece[1] for piece in code]))

    rates = 1.0 / spans.T
    weight = residues.T * jnp.sqrt(rates) * (1.0 / SCALE)
    decay = jnp.exp(-rates)
    sub_index = jnp.arange(SUBS, dtype=jnp.int32)

    def first_token(side):
        return (2 * span_tokens * (sub_index // 2) + steps * (sub_index % 2) + span_tokens * side).astype(F32)[None, :, None]

    def tail(side):
        return jnp.exp(-rates[:, None, :] * (tokens - steps - first_token(side)))

    def start(side):
        return weight[:, None, :] * jnp.exp(-rates[:, None, :] * (first_token(side) + 1.0))

    def states(code, tail, earlier):
        return pl.pallas_call(
            functools.partial(state_kernel, modes),
            in_specs=[VMEM] * 4,
            out_specs=[VMEM] * 3,
            out_shape=[
                jax.ShapeDtypeStruct((groups, half, LANES), F32),
                jax.ShapeDtypeStruct((modes, SUBS, channels), F32),
                jax.ShapeDtypeStruct((modes, channels), F32),
            ],
            compiler_params=PARAMS,
            cost_estimate=pl.CostEstimate(flops=1000, bytes_accessed=1000, transcendentals=0),
        )(code, decay, tail, earlier)

    near_drive, near_subs, block = states(near_code, tail(core), jnp.zeros((modes, channels), F32))
    far_drive, far_subs, block = states(far_code, tail(1 - core), block)
    rates, weight, block = lax.optimization_barrier((rates, weight, block))
    step_decay = jnp.exp(-rates * steps)

    local = [
        pl.pallas_call(
            functools.partial(local_kernel, modes, begin),
            in_specs=[VMEM] * 8,
            out_specs=[VMEM] * 2,
            out_shape=[jax.ShapeDtypeStruct((groups // 2, half, LANES), F32)] * 2,
            compiler_params=PARAMS,
            cost_estimate=pl.CostEstimate(flops=40_000_000, bytes_accessed=4_000_000, transcendentals=0),
        )(
            near_drive, far_drive, near_subs, far_subs, decay, step_decay, weight,
            skip.reshape(1, channels) * (1.0 / SCALE),
        )
        for begin in (0, groups // 2)
    ]

    index = lax.axis_index("ctx")
    col, row = index % 4, index // 4

    def power(count):
        count = jnp.asarray(count)
        return jnp.where(count >= 0, jnp.exp(-rates * jnp.maximum(count, 0).astype(F32)), 0.0)

    near_start, far_start = start(core), start(1 - core)

    def final(carry, out=None):
        early = out is None
        return pl.pallas_call(
            functools.partial(final_kernel, modes, early),
            in_specs=[VMEM] * 9 + [pl.BlockSpec(memory_space=pl.ANY)] * (not early),
            out_specs=pl.BlockSpec(memory_space=pl.ANY),
            out_shape=jax.ShapeDtypeStruct((channels, tokens), BF16),
            input_output_aliases={} if early else {9: 0},
            scratch_shapes=[
                pltpu.VMEM((2, groups, half, LANES), F32),
                pltpu.VMEM((groups, LANES, tokens), BF16),
                pltpu.SemaphoreType.DMA((groups,)),
            ],
            compiler_params=PARAMS,
        )(*local[0], *local[1], query, carry, near_start, far_start, decay, *(() if early else (out,)))

    others = [across_blocks(block, k) for k in CHIP_ORDER]
    others, query, local = lax.optimization_barrier((others, query, local))
    before = jnp.zeros_like(block)
    total = power(tokens * (3 - col)) * block
    for k, other in zip(CHIP_ORDER, others):
        before = before + power(tokens * (col - 1 - (col ^ k))) * other
        total = total + power(tokens * (3 - (col ^ k))) * other
    total, out = lax.optimization_barrier((total, final(before)))
    others = [across_blocks(total, 4 * k) for k in CHIP_ORDER]
    carry = jnp.zeros_like(block)
    for k, other in zip(CHIP_ORDER, others):
        carry = carry + power(4 * tokens * (row - 1 - (row ^ k))) * other
    return final(before + power(tokens * col) * carry, out)


def solution(mesh):
    return jax.shard_map(
        per_device,
        mesh=mesh,
        in_specs=(P(None, ("ctx", "tp"), None), P("tp", None), P("tp", None), P("tp")),
        out_specs=P("tp", "ctx"),
        check_vma=False,
    )
```

```python
import functools

import jax
import jax.numpy as jnp
from jax import lax
from jax.experimental import pallas as pl
from jax.experimental.pallas import tpu as pltpu
from jax.sharding import PartitionSpec as P

F32 = jnp.float32
BF16 = jnp.bfloat16
SUBS = 8
LANES = 128
SCALE = 1024.0
OPEN_VMEM = 52 * 1024 * 1024
CHIP_ORDER = (2, 1, 3)
COL_ORDER = (2, 3, 1)
ROW_ORDER = (2, 3, 1)
VMEM = pl.BlockSpec(memory_space=pltpu.VMEM)
PARAMS = pltpu.CompilerParams(vmem_limit_bytes=32 * 1024 * 1024)


def encode(scaled):
    size = jnp.maximum(jnp.abs(scaled), 1.0)
    square = size * size
    return (scaled * (square * square * square * size)).astype(BF16)


def decode(code):
    code = code.astype(F32)
    half = lax.rsqrt(jnp.maximum(jnp.abs(code), 1.0))
    eighth = lax.rsqrt(lax.rsqrt(half))
    return code * (half * eighth * eighth * eighth)


def open_kernel(qkv_ref, *refs):
    *code_refs, held_ref, held_sem = refs
    _, _, width = code_refs[0].shape
    place = lax.axis_index("tp")

    def fetch(k):
        lanes = pl.ds(pl.multiple_of((place // 2 ^ k) * 2 * width, 2 * width), 2 * width)
        return pltpu.make_async_copy(qkv_ref.at[pl.ds(1, 2), :, lanes], held_ref.at[k], held_sem.at[k])

    order = CHIP_ORDER + (0,)
    for k in order:
        fetch(k).start()
    for k in order:
        fetch(k).wait()
        for flip in range(2):
            half = pl.ds(pl.multiple_of((place % 2 ^ flip) * width, width), width)
            scaled = held_ref[k, 0, :, half].astype(F32) * held_ref[k, 1, :, half].astype(F32) * SCALE
            code_refs[k][flip] = encode(scaled)


def query_kernel(qkv_ref, query_ref, moved_ref, sem):
    parts, _, width = moved_ref.shape
    copies = [pltpu.make_async_copy(moved_ref.at[part], query_ref.at[part], sem.at[part]) for part in range(parts)]
    for part in range(parts):
        moved_ref[part] = qkv_ref[0, :, pl.ds(part * width, width)]
        copies[part].start()
    for copy in copies:
        copy.wait()


def across_core(value):
    return lax.ppermute(value, "tp", [(i, i ^ 1) for i in range(lax.axis_size("tp"))])


def across_chips(value, k):
    return lax.ppermute(value, "tp", [(i, i ^ 2 * k) for i in range(lax.axis_size("tp"))])


def across_blocks(value, bits):
    return lax.ppermute(value, "ctx", [(i, i ^ bits) for i in range(lax.axis_size("ctx"))])


def wide(ref, mode, lanes):
    return jnp.broadcast_to(ref[mode : mode + 1, lanes], (SUBS, LANES))


def total_of(parts):
    while len(parts) > 1:
        parts = [parts[j] + parts[j + 1] if j + 1 < len(parts) else parts[j] for j in range(0, len(parts), 2)]
    return parts[0]


def state_kernel(modes, code_ref, decay_ref, tail_ref, earlier_ref, drive_ref, sub_ref, block_ref):
    chips, tokens, channels = code_ref.shape
    steps = chips * tokens // SUBS
    chip = lax.axis_index("tp") // 2
    for source in range(chips):
        k = chip ^ source
        slot = k % 2 * 2 + k // 2
        for group in range(channels // LANES):
            lanes = pl.ds(group * LANES, LANES)
            drive = decode(code_ref[slot, :, lanes])
            for sub in range(SUBS * source // chips, SUBS * (source + 1) // chips):
                at = sub * steps - source * tokens
                drive_ref[group, pl.ds(sub, steps, stride=SUBS), :] = drive[at : at + steps]
    for group in range(channels // LANES):
        lanes = pl.ds(group * LANES, LANES)
        decay = [wide(decay_ref, mode, lanes) for mode in range(modes)]

        def step(i, states):
            x = drive_ref[group, pl.ds(pl.multiple_of(i * SUBS, SUBS), SUBS), :]
            return [states[m] * decay[m] + x for m in range(modes)]

        zero = jnp.zeros((SUBS, LANES), F32)
        states = lax.fori_loop(0, steps, step, [zero] * modes, unroll=steps)
        for mode in range(modes):
            sub_ref[mode, :, lanes] = states[mode]
            block_ref[mode : mode + 1, lanes] = earlier_ref[mode : mode + 1, lanes] + jnp.sum(
                states[mode] * tail_ref[mode, :, lanes], axis=0, keepdims=True
            )


def first_states(near, far, decay_32, core):
    row = lax.broadcasted_iota(jnp.int32, (SUBS, LANES), 0)
    odd = row % 2 == 1
    decay_64 = decay_32 * decay_32
    decay_128 = decay_64 * decay_64
    first = jnp.where(core == 0, near, far)
    second = jnp.where(core == 0, far, near)
    first_before, second_before = pltpu.roll(first, 1, 0), pltpu.roll(second, 1, 0)
    first_whole = first + decay_32 * first_before
    held = second + decay_32 * second_before + decay_64 * first_whole
    held = held + decay_128 * jnp.where(row >= 2, pltpu.roll(held, 2, 0), 0.0)
    held = held + decay_128 * decay_128 * jnp.where(row >= 4, pltpu.roll(held, 4, 0), 0.0)
    into = jnp.where(odd, pltpu.roll(held, 2, 0), pltpu.roll(held, 1, 0))
    into = jnp.where(row >= 2, into, 0.0)
    middle = decay_64 * into + jnp.where(odd, first_whole, pltpu.roll(first_whole, SUBS - 1, 0))
    first = jnp.where(odd, decay_32 * into + first_before, into)
    second = jnp.where(odd, decay_32 * middle + second_before, middle)
    return jnp.where(core == 0, first, second), jnp.where(core == 0, second, first)


def local_kernel(modes, begin, *refs):
    drive_refs, (near_ref, far_ref, decay_ref, step_decay_ref, weight_ref, skip_ref), out_refs = refs[:2], refs[2:8], refs[8:]
    groups, tokens, _ = out_refs[0].shape
    steps = tokens // SUBS
    core = lax.axis_index("tp") % 2
    for group in range(groups):
        lanes = pl.ds((begin + group) * LANES, LANES)
        decay = [wide(decay_ref, mode, lanes) for mode in range(modes)]
        weight = [wide(weight_ref, mode, lanes) for mode in range(modes)]
        skip = jnp.broadcast_to(skip_ref[0:1, lanes], (SUBS, LANES))
        starts = [
            first_states(near_ref[m, :, lanes], far_ref[m, :, lanes], wide(step_decay_ref, m, lanes), core)
            for m in range(modes)
        ]
        for part, (drive_ref, out_ref) in enumerate(zip(drive_refs, out_refs)):

            def step(i, states):
                at = pl.ds(pl.multiple_of(i * SUBS, SUBS), SUBS)
                x = drive_ref[begin + group, at, :]
                states = [states[m] * decay[m] + x for m in range(modes)]
                out_ref[group, at, :] = total_of([states[m] * weight[m] for m in range(modes)] + [skip * x])
                return states

            lax.fori_loop(0, steps, step, [start[part] for start in starts], unroll=8)


def final_kernel(modes, early, *refs):
    row = lax.axis_index("ctx") // 4

    @pl.when(row == 0 if early else row > 0)
    def _():
        finish(modes, *refs[: 9], *refs[9 if early else 10 :])


def finish(modes, *refs):
    low_refs, high_refs = refs[0:2], refs[2:4]
    query_ref, carry_ref, near_ref, far_ref, decay_ref, out_ref, sum_ref, held_ref, out_sem = refs[4:]
    _, groups, tokens, _ = sum_ref.shape
    steps = tokens // SUBS
    core = lax.axis_index("tp") % 2

    def copy_out(group):
        return pltpu.make_async_copy(held_ref.at[group], out_ref.at[pl.ds(group * LANES, LANES)], out_sem.at[group])

    for group in range(groups):
        lanes = pl.ds(group * LANES, LANES)
        decay = [wide(decay_ref, mode, lanes) for mode in range(modes)]
        local_refs = low_refs if group < groups // 2 else high_refs
        for part, start_ref in enumerate((near_ref, far_ref)):
            local_ref = local_refs[part]
            first = [start_ref[mode, :, lanes] * wide(carry_ref, mode, lanes) for mode in range(modes)]

            def step(i, states):
                at = pl.ds(pl.multiple_of(i * SUBS, SUBS), SUBS)
                sum_ref[core ^ part, group, at, :] = total_of([local_ref[group % (groups // 2), at, :]] + states)
                return [states[m] * decay[m] for m in range(modes)]

            lax.fori_loop(0, steps, step, first, unroll=steps)
        for tile in range(2 * tokens // LANES):
            rows = pl.ds(tile * LANES, LANES)
            subs = [sum_ref[part, group, pl.ds(2 * tile + j, steps, stride=SUBS), :] for part in range(2) for j in range(2)]
            mixed = jnp.concatenate(subs)
            gated = mixed * query_ref[rows, lanes].astype(F32)
            held_ref[group, :, rows] = gated.T.astype(BF16)
        copy_out(group).start()
    for group in range(groups):
        copy_out(group).wait()


def per_device(qkv, residues, spans, skip):
    _, span_tokens, _ = qkv.shape
    devices = lax.axis_size("tp")
    chips = devices // 2
    channels, modes = residues.shape
    tokens = devices * span_tokens
    half = tokens // 2
    groups = channels // LANES
    steps = half // SUBS
    core = lax.axis_index("tp") % 2

    code = list(
        pl.pallas_call(
            open_kernel,
            in_specs=[pl.BlockSpec(memory_space=pl.ANY)],
            out_specs=[VMEM] * chips,
            out_shape=[jax.ShapeDtypeStruct((2, span_tokens, channels), BF16)] * chips,
            scratch_shapes=[
                pltpu.VMEM((chips, 2, span_tokens, 2 * channels), BF16),
                pltpu.SemaphoreType.DMA((chips,)),
            ],
            compiler_params=pltpu.CompilerParams(vmem_limit_bytes=OPEN_VMEM),
        )(qkv)
    )
    query = pl.pallas_call(
        query_kernel,
        in_specs=[VMEM],
        out_specs=pl.BlockSpec(memory_space=pl.ANY),
        out_shape=jax.ShapeDtypeStruct((devices, span_tokens, channels), BF16),
        scratch_shapes=[pltpu.VMEM((devices, span_tokens, channels), BF16), pltpu.SemaphoreType.DMA((devices,))],
        compiler_params=PARAMS,
    )(qkv)
    for k in CHIP_ORDER:
        code[k] = across_chips(code[k], k)
    query = lax.all_to_all(query, "tp", 0, 0).reshape(tokens, channels)
    code = [code[0]] + [code[k] for k in CHIP_ORDER]
    near_code = jnp.stack([piece[0] for piece in code])
    far_code = across_core(jnp.stack([piece[1] for piece in code]))

    rates = 1.0 / spans.T
    weight = residues.T * jnp.sqrt(rates) * (1.0 / SCALE)
    decay = jnp.exp(-rates)
    sub_index = jnp.arange(SUBS, dtype=jnp.int32)

    def first_token(side):
        return (2 * span_tokens * (sub_index // 2) + steps * (sub_index % 2) + span_tokens * side).astype(F32)[None, :, None]

    def tail(side):
        return jnp.exp(-rates[:, None, :] * (tokens - steps - first_token(side)))

    def start(side):
        return weight[:, None, :] * jnp.exp(-rates[:, None, :] * (first_token(side) + 1.0))

    def states(code, tail, earlier):
        return pl.pallas_call(
            functools.partial(state_kernel, modes),
            in_specs=[VMEM] * 4,
            out_specs=[VMEM] * 3,
            out_shape=[
                jax.ShapeDtypeStruct((groups, half, LANES), F32),
                jax.ShapeDtypeStruct((modes, SUBS, channels), F32),
                jax.ShapeDtypeStruct((modes, channels), F32),
            ],
            compiler_params=PARAMS,
            cost_estimate=pl.CostEstimate(flops=1000, bytes_accessed=1000, transcendentals=0),
        )(code, decay, tail, earlier)

    near_drive, near_subs, block = states(near_code, tail(core), jnp.zeros((modes, channels), F32))
    far_drive, far_subs, block = states(far_code, tail(1 - core), block)
    rates, weight, block = lax.optimization_barrier((rates, weight, block))
    step_decay = jnp.exp(-rates * steps)

    local = [
        pl.pallas_call(
            functools.partial(local_kernel, modes, begin),
            in_specs=[VMEM] * 8,
            out_specs=[VMEM] * 2,
            out_shape=[jax.ShapeDtypeStruct((groups // 2, half, LANES), F32)] * 2,
            compiler_params=PARAMS,
            cost_estimate=pl.CostEstimate(flops=40_000_000, bytes_accessed=4_000_000, transcendentals=0),
        )(
            near_drive, far_drive, near_subs, far_subs, decay, step_decay, weight,
            skip.reshape(1, channels) * (1.0 / SCALE),
        )
        for begin in (0, groups // 2)
    ]

    index = lax.axis_index("ctx")
    col, row = index % 4, index // 4

    def power(count):
        count = jnp.asarray(count)
        return jnp.where(count >= 0, jnp.exp(-rates * jnp.maximum(count, 0).astype(F32)), 0.0)

    near_start, far_start = start(core), start(1 - core)

    def final(carry, out=None):
        early = out is None
        return pl.pallas_call(
            functools.partial(final_kernel, modes, early),
            in_specs=[VMEM] * 9 + [pl.BlockSpec(memory_space=pl.ANY)] * (not early),
            out_specs=pl.BlockSpec(memory_space=pl.ANY),
            out_shape=jax.ShapeDtypeStruct((channels, tokens), BF16),
            input_output_aliases={} if early else {9: 0},
            scratch_shapes=[
                pltpu.VMEM((2, groups, half, LANES), F32),
                pltpu.VMEM((groups, LANES, tokens), BF16),
                pltpu.SemaphoreType.DMA((groups,)),
            ],
            compiler_params=PARAMS,
        )(*local[0], *local[1], query, carry, near_start, far_start, decay, *(() if early else (out,)))

    others = [across_blocks(block, k) for k in COL_ORDER]
    others, query, local = lax.optimization_barrier((others, query, local))
    before = jnp.zeros_like(block)
    total = power(tokens * (3 - col)) * block
    for k, other in zip(COL_ORDER, others):
        before = before + power(tokens * (col - 1 - (col ^ k))) * other
        total = total + power(tokens * (3 - (col ^ k))) * other
    total, out = lax.optimization_barrier((total, final(before)))
    others = [across_blocks(total, 4 * k) for k in ROW_ORDER]
    carry = jnp.zeros_like(block)
    for k, other in zip(ROW_ORDER, others):
        carry = carry + power(4 * tokens * (row - 1 - (row ^ k))) * other
    return final(before + power(tokens * col) * carry, out)


def solution(mesh):
    return jax.shard_map(
        per_device,
        mesh=mesh,
        in_specs=(P(None, ("ctx", "tp"), None), P("tp", None), P("tp", None), P("tp")),
        out_specs=P("tp", "ctx"),
        check_vma=False,
    )
```

```python
import functools

import jax
import jax.numpy as jnp
from jax import lax
from jax.experimental import pallas as pl
from jax.experimental.pallas import tpu as pltpu
from jax.sharding import PartitionSpec as P

F32 = jnp.float32
BF16 = jnp.bfloat16
SUBS = 8
LANES = 128
SCALE = 1024.0
OPEN_VMEM = 52 * 1024 * 1024
CHIP_ORDER = (2, 1, 3)
COL_ORDER = (2, 3, 1)
ROW_ORDER = (2, 3, 1)
VMEM = pl.BlockSpec(memory_space=pltpu.VMEM)
PARAMS = pltpu.CompilerParams(vmem_limit_bytes=32 * 1024 * 1024)


def encode(scaled):
    size = jnp.maximum(jnp.abs(scaled), 1.0)
    square = size * size
    return (scaled * (square * square * square * size)).astype(BF16)


def decode(code):
    code = code.astype(F32)
    half = lax.rsqrt(jnp.maximum(jnp.abs(code), 1.0))
    eighth = lax.rsqrt(lax.rsqrt(half))
    return code * (half * eighth * eighth * eighth)


def open_kernel(qkv_ref, *refs):
    *code_refs, held_ref, held_sem = refs
    _, _, width = code_refs[0].shape
    place = lax.axis_index("tp")

    def fetch(k):
        lanes = pl.ds(pl.multiple_of((place // 2 ^ k) * 2 * width, 2 * width), 2 * width)
        return pltpu.make_async_copy(qkv_ref.at[pl.ds(1, 2), :, lanes], held_ref.at[k], held_sem.at[k])

    order = CHIP_ORDER + (0,)
    for k in order:
        fetch(k).start()
    for k in order:
        fetch(k).wait()
        for flip in range(2):
            half = pl.ds(pl.multiple_of((place % 2 ^ flip) * width, width), width)
            scaled = held_ref[k, 0, :, half].astype(F32) * held_ref[k, 1, :, half].astype(F32) * SCALE
            code_refs[k][flip] = encode(scaled)


def query_kernel(qkv_ref, query_ref, moved_ref, sem):
    parts, _, width = moved_ref.shape
    copies = [pltpu.make_async_copy(moved_ref.at[part], query_ref.at[part], sem.at[part]) for part in range(parts)]
    for part in range(parts):
        moved_ref[part] = qkv_ref[0, :, pl.ds(part * width, width)]
        copies[part].start()
    for copy in copies:
        copy.wait()


def across_core(value):
    return lax.ppermute(value, "tp", [(i, i ^ 1) for i in range(lax.axis_size("tp"))])


def across_chips(value, k):
    return lax.ppermute(value, "tp", [(i, i ^ 2 * k) for i in range(lax.axis_size("tp"))])


def across_blocks(value, bits):
    return lax.ppermute(value, "ctx", [(i, i ^ bits) for i in range(lax.axis_size("ctx"))])


def wide(ref, mode, lanes):
    return jnp.broadcast_to(ref[mode : mode + 1, lanes], (SUBS, LANES))


def total_of(parts):
    while len(parts) > 1:
        parts = [parts[j] + parts[j + 1] if j + 1 < len(parts) else parts[j] for j in range(0, len(parts), 2)]
    return parts[0]


def state_kernel(modes, code_ref, decay_ref, tail_ref, earlier_ref, drive_ref, sub_ref, block_ref):
    chips, tokens, channels = code_ref.shape
    steps = chips * tokens // SUBS
    chip = lax.axis_index("tp") // 2
    for source in range(chips):
        k = chip ^ source
        slot = k % 2 * 2 + k // 2
        for group in range(channels // LANES):
            lanes = pl.ds(group * LANES, LANES)
            drive = decode(code_ref[slot, :, lanes])
            for sub in range(SUBS * source // chips, SUBS * (source + 1) // chips):
                at = sub * steps - source * tokens
                drive_ref[group, pl.ds(sub, steps, stride=SUBS), :] = drive[at : at + steps]
    for group in range(channels // LANES):
        lanes = pl.ds(group * LANES, LANES)
        decay = [wide(decay_ref, mode, lanes) for mode in range(modes)]

        def step(i, states):
            x = drive_ref[group, pl.ds(pl.multiple_of(i * SUBS, SUBS), SUBS), :]
            return [states[m] * decay[m] + x for m in range(modes)]

        zero = jnp.zeros((SUBS, LANES), F32)
        states = lax.fori_loop(0, steps, step, [zero] * modes, unroll=steps)
        for mode in range(modes):
            sub_ref[mode, :, lanes] = states[mode]
            block_ref[mode : mode + 1, lanes] = earlier_ref[mode : mode + 1, lanes] + jnp.sum(
                states[mode] * tail_ref[mode, :, lanes], axis=0, keepdims=True
            )


def first_states(near, far, decay_32, core):
    row = lax.broadcasted_iota(jnp.int32, (SUBS, LANES), 0)
    odd = row % 2 == 1
    decay_64 = decay_32 * decay_32
    decay_128 = decay_64 * decay_64
    first = jnp.where(core == 0, near, far)
    second = jnp.where(core == 0, far, near)
    first_before, second_before = pltpu.roll(first, 1, 0), pltpu.roll(second, 1, 0)
    first_whole = first + decay_32 * first_before
    held = second + decay_32 * second_before + decay_64 * first_whole
    held = held + decay_128 * jnp.where(row >= 2, pltpu.roll(held, 2, 0), 0.0)
    held = held + decay_128 * decay_128 * jnp.where(row >= 4, pltpu.roll(held, 4, 0), 0.0)
    into = jnp.where(odd, pltpu.roll(held, 2, 0), pltpu.roll(held, 1, 0))
    into = jnp.where(row >= 2, into, 0.0)
    middle = decay_64 * into + jnp.where(odd, first_whole, pltpu.roll(first_whole, SUBS - 1, 0))
    first = jnp.where(odd, decay_32 * into + first_before, into)
    second = jnp.where(odd, decay_32 * middle + second_before, middle)
    return jnp.where(core == 0, first, second), jnp.where(core == 0, second, first)


def local_kernel(modes, begin, *refs):
    drive_refs, (near_ref, far_ref, decay_ref, step_decay_ref, weight_ref, skip_ref), out_refs = refs[:2], refs[2:8], refs[8:]
    groups, tokens, _ = out_refs[0].shape
    steps = tokens // SUBS
    core = lax.axis_index("tp") % 2
    for group in range(groups):
        lanes = pl.ds((begin + group) * LANES, LANES)
        decay = [wide(decay_ref, mode, lanes) for mode in range(modes)]
        weight = [wide(weight_ref, mode, lanes) for mode in range(modes)]
        skip = jnp.broadcast_to(skip_ref[0:1, lanes], (SUBS, LANES))
        starts = [
            first_states(near_ref[m, :, lanes], far_ref[m, :, lanes], wide(step_decay_ref, m, lanes), core)
            for m in range(modes)
        ]
        for part, (drive_ref, out_ref) in enumerate(zip(drive_refs, out_refs)):

            def step(i, states):
                at = pl.ds(pl.multiple_of(i * SUBS, SUBS), SUBS)
                x = drive_ref[begin + group, at, :]
                states = [states[m] * decay[m] + x for m in range(modes)]
                out_ref[group, at, :] = total_of([states[m] * weight[m] for m in range(modes)] + [skip * x])
                return states

            lax.fori_loop(0, steps, step, [start[part] for start in starts], unroll=8)


def final_kernel(modes, early, *refs):
    row = lax.axis_index("ctx") // 4

    @pl.when(row == 0 if early else row > 0)
    def _():
        finish(modes, *refs[: 9], *refs[9 if early else 10 :])


def finish(modes, *refs):
    low_refs, high_refs = refs[0:2], refs[2:4]
    query_ref, carry_ref, near_ref, far_ref, decay_ref, out_ref, sum_ref, held_ref, out_sem = refs[4:]
    _, groups, tokens, _ = sum_ref.shape
    steps = tokens // SUBS
    core = lax.axis_index("tp") % 2

    def copy_out(group):
        return pltpu.make_async_copy(held_ref.at[group], out_ref.at[pl.ds(group * LANES, LANES)], out_sem.at[group])

    for group in range(groups):
        lanes = pl.ds(group * LANES, LANES)
        decay = [wide(decay_ref, mode, lanes) for mode in range(modes)]
        local_refs = low_refs if group < groups // 2 else high_refs
        for part, start_ref in enumerate((near_ref, far_ref)):
            local_ref = local_refs[part]
            first = [start_ref[mode, :, lanes] * wide(carry_ref, mode, lanes) for mode in range(modes)]

            def step(i, states):
                at = pl.ds(pl.multiple_of(i * SUBS, SUBS), SUBS)
                sum_ref[core ^ part, group, at, :] = total_of([local_ref[group % (groups // 2), at, :]] + states)
                return [states[m] * decay[m] for m in range(modes)]

            lax.fori_loop(0, steps, step, first, unroll=steps)
        for tile in range(2 * tokens // LANES):
            rows = pl.ds(tile * LANES, LANES)
            subs = [sum_ref[part, group, pl.ds(2 * tile + j, steps, stride=SUBS), :] for part in range(2) for j in range(2)]
            mixed = jnp.concatenate(subs)
            gated = mixed * query_ref[rows, lanes].astype(F32)
            held_ref[group, :, rows] = gated.T.astype(BF16)
        copy_out(group).start()
    for group in range(groups):
        copy_out(group).wait()


def per_device(qkv, residues, spans, skip):
    _, span_tokens, _ = qkv.shape
    devices = lax.axis_size("tp")
    chips = devices // 2
    channels, modes = residues.shape
    tokens = devices * span_tokens
    half = tokens // 2
    groups = channels // LANES
    steps = half // SUBS
    core = lax.axis_index("tp") % 2

    code = list(
        pl.pallas_call(
            open_kernel,
            in_specs=[pl.BlockSpec(memory_space=pl.ANY)],
            out_specs=[VMEM] * chips,
            out_shape=[jax.ShapeDtypeStruct((2, span_tokens, channels), BF16)] * chips,
            scratch_shapes=[
                pltpu.VMEM((chips, 2, span_tokens, 2 * channels), BF16),
                pltpu.SemaphoreType.DMA((chips,)),
            ],
            compiler_params=pltpu.CompilerParams(vmem_limit_bytes=OPEN_VMEM),
        )(qkv)
    )
    query = pl.pallas_call(
        query_kernel,
        in_specs=[VMEM],
        out_specs=pl.BlockSpec(memory_space=pl.ANY),
        out_shape=jax.ShapeDtypeStruct((devices, span_tokens, channels), BF16),
        scratch_shapes=[pltpu.VMEM((devices, span_tokens, channels), BF16), pltpu.SemaphoreType.DMA((devices,))],
        compiler_params=PARAMS,
    )(qkv)
    for k in CHIP_ORDER:
        code[k] = across_chips(code[k], k)
    query = lax.all_to_all(query, "tp", 0, 0).reshape(tokens, channels)
    code = [code[0]] + [code[k] for k in CHIP_ORDER]
    near_code = jnp.stack([piece[0] for piece in code])
    far_code = across_core(jnp.stack([piece[1] for piece in code]))

    rates = 1.0 / spans.T
    weight = residues.T * jnp.sqrt(rates) * (1.0 / SCALE)
    decay = jnp.exp(-rates)
    sub_index = jnp.arange(SUBS, dtype=jnp.int32)

    def first_token(side):
        return (2 * span_tokens * (sub_index // 2) + steps * (sub_index % 2) + span_tokens * side).astype(F32)[None, :, None]

    def tail(side):
        return jnp.exp(-rates[:, None, :] * (tokens - steps - first_token(side)))

    def start(side):
        return weight[:, None, :] * jnp.exp(-rates[:, None, :] * (first_token(side) + 1.0))

    def states(code, tail, earlier):
        return pl.pallas_call(
            functools.partial(state_kernel, modes),
            in_specs=[VMEM] * 4,
            out_specs=[VMEM] * 3,
            out_shape=[
                jax.ShapeDtypeStruct((groups, half, LANES), F32),
                jax.ShapeDtypeStruct((modes, SUBS, channels), F32),
                jax.ShapeDtypeStruct((modes, channels), F32),
            ],
            compiler_params=PARAMS,
            cost_estimate=pl.CostEstimate(flops=1000, bytes_accessed=1000, transcendentals=0),
        )(code, decay, tail, earlier)

    near_drive, near_subs, block = states(near_code, tail(core), jnp.zeros((modes, channels), F32))
    far_drive, far_subs, block = states(far_code, tail(1 - core), block)
    rates, weight, block = lax.optimization_barrier((rates, weight, block))
    step_decay = jnp.exp(-rates * steps)

    local = [
        pl.pallas_call(
            functools.partial(local_kernel, modes, begin),
            in_specs=[VMEM] * 8,
            out_specs=[VMEM] * 2,
            out_shape=[jax.ShapeDtypeStruct((groups // 2, half, LANES), F32)] * 2,
            compiler_params=PARAMS,
            cost_estimate=pl.CostEstimate(flops=40_000_000, bytes_accessed=4_000_000, transcendentals=0),
        )(
            near_drive, far_drive, near_subs, far_subs, decay, step_decay, weight,
            skip.reshape(1, channels) * (1.0 / SCALE),
        )
        for begin in (0, groups // 2)
    ]

    index = lax.axis_index("ctx")
    col, row = index % 4, index // 4

    def power(count):
        count = jnp.asarray(count)
        return jnp.where(count >= 0, jnp.exp(-rates * jnp.maximum(count, 0).astype(F32)), 0.0)

    near_start, far_start = start(core), start(1 - core)

    def final(carry, out=None):
        early = out is None
        return pl.pallas_call(
            functools.partial(final_kernel, modes, early),
            in_specs=[VMEM] * 9 + [pl.BlockSpec(memory_space=pl.ANY)] * (not early),
            out_specs=pl.BlockSpec(memory_space=pl.ANY),
            out_shape=jax.ShapeDtypeStruct((channels, tokens), BF16),
            input_output_aliases={} if early else {9: 0},
            scratch_shapes=[
                pltpu.VMEM((2, groups, half, LANES), F32),
                pltpu.VMEM((groups, LANES, tokens), BF16),
                pltpu.SemaphoreType.DMA((groups,)),
            ],
            compiler_params=PARAMS,
        )(*local[0], *local[1], query, carry, near_start, far_start, decay, *(() if early else (out,)))

    others = [across_blocks(block, k) for k in COL_ORDER]
    others, query, local = lax.optimization_barrier((others, query, local))
    before = jnp.zeros_like(block)
    total = power(tokens * (3 - col)) * block
    for k, other in zip(COL_ORDER, others):
        before = before + power(tokens * (col - 1 - (col ^ k))) * other
        total = total + power(tokens * (3 - (col ^ k))) * other
    others = [across_blocks(total, 4 * k) for k in ROW_ORDER]
    others, out = lax.optimization_barrier((others, final(before)))
    carry = jnp.zeros_like(block)
    for k, other in zip(ROW_ORDER, others):
        carry = carry + power(4 * tokens * (row - 1 - (row ^ k))) * other
    return final(before + power(tokens * col) * carry, out)


def solution(mesh):
    return jax.shard_map(
        per_device,
        mesh=mesh,
        in_specs=(P(None, ("ctx", "tp"), None), P("tp", None), P("tp", None), P("tp")),
        out_specs=P("tp", "ctx"),
        check_vma=False,
    )
```

```python
import functools

import jax
import jax.numpy as jnp
from jax import lax
from jax.experimental import pallas as pl
from jax.experimental.pallas import tpu as pltpu
from jax.sharding import PartitionSpec as P

F32 = jnp.float32
BF16 = jnp.bfloat16
SUBS = 8
LANES = 128
SCALE = 1024.0
OPEN_VMEM = 52 * 1024 * 1024
CHIP_ORDER = (2, 1, 3)
COL_ORDER = (2, 3, 1)
ROW_ORDER = (2, 3, 1)
VMEM = pl.BlockSpec(memory_space=pltpu.VMEM)
PARAMS = pltpu.CompilerParams(vmem_limit_bytes=32 * 1024 * 1024)


def encode(scaled):
    size = jnp.maximum(jnp.abs(scaled), 1.0)
    square = size * size
    return (scaled * (square * square * square * size)).astype(BF16)


def decode(code):
    code = code.astype(F32)
    half = lax.rsqrt(jnp.maximum(jnp.abs(code), 1.0))
    eighth = lax.rsqrt(lax.rsqrt(half))
    return code * (half * eighth * eighth * eighth)


def open_kernel(qkv_ref, *refs):
    *code_refs, held_ref, held_sem = refs
    _, _, width = code_refs[0].shape
    place = lax.axis_index("tp")

    def fetch(k):
        lanes = pl.ds(pl.multiple_of((place // 2 ^ k) * 2 * width, 2 * width), 2 * width)
        return pltpu.make_async_copy(qkv_ref.at[pl.ds(1, 2), :, lanes], held_ref.at[k], held_sem.at[k])

    order = CHIP_ORDER + (0,)
    for k in order:
        fetch(k).start()
    for k in order:
        fetch(k).wait()
        for flip in range(2):
            half = pl.ds(pl.multiple_of((place % 2 ^ flip) * width, width), width)
            scaled = held_ref[k, 0, :, half].astype(F32) * held_ref[k, 1, :, half].astype(F32) * SCALE
            code_refs[k][flip] = encode(scaled)


def query_kernel(qkv_ref, query_ref, moved_ref, sem):
    parts, _, width = moved_ref.shape
    copies = [pltpu.make_async_copy(moved_ref.at[part], query_ref.at[part], sem.at[part]) for part in range(parts)]
    for part in range(parts):
        moved_ref[part] = qkv_ref[0, :, pl.ds(part * width, width)]
        copies[part].start()
    for copy in copies:
        copy.wait()


def across_core(value):
    return lax.ppermute(value, "tp", [(i, i ^ 1) for i in range(lax.axis_size("tp"))])


def across_chips(value, k):
    return lax.ppermute(value, "tp", [(i, i ^ 2 * k) for i in range(lax.axis_size("tp"))])


def across_blocks(value, bits):
    return lax.ppermute(value, "ctx", [(i, i ^ bits) for i in range(lax.axis_size("ctx"))])


def wide(ref, mode, lanes):
    return jnp.broadcast_to(ref[mode : mode + 1, lanes], (SUBS, LANES))


def total_of(parts):
    while len(parts) > 1:
        parts = [parts[j] + parts[j + 1] if j + 1 < len(parts) else parts[j] for j in range(0, len(parts), 2)]
    return parts[0]


def state_kernel(modes, code_ref, decay_ref, tail_ref, earlier_ref, drive_ref, sub_ref, block_ref):
    chips, tokens, channels = code_ref.shape
    steps = chips * tokens // SUBS
    chip = lax.axis_index("tp") // 2
    for source in range(chips):
        k = chip ^ source
        slot = k % 2 * 2 + k // 2
        for group in range(channels // LANES):
            lanes = pl.ds(group * LANES, LANES)
            drive = decode(code_ref[slot, :, lanes])
            for sub in range(SUBS * source // chips, SUBS * (source + 1) // chips):
                at = sub * steps - source * tokens
                drive_ref[group, pl.ds(sub, steps, stride=SUBS), :] = drive[at : at + steps]
    for group in range(channels // LANES):
        lanes = pl.ds(group * LANES, LANES)
        decay = [wide(decay_ref, mode, lanes) for mode in range(modes)]

        def step(i, states):
            x = drive_ref[group, pl.ds(pl.multiple_of(i * SUBS, SUBS), SUBS), :]
            return [states[m] * decay[m] + x for m in range(modes)]

        zero = jnp.zeros((SUBS, LANES), F32)
        states = lax.fori_loop(0, steps, step, [zero] * modes, unroll=steps)
        for mode in range(modes):
            sub_ref[mode, :, lanes] = states[mode]
            block_ref[mode : mode + 1, lanes] = earlier_ref[mode : mode + 1, lanes] + jnp.sum(
                states[mode] * tail_ref[mode, :, lanes], axis=0, keepdims=True
            )


def first_states(near, far, decay_32, core):
    row = lax.broadcasted_iota(jnp.int32, (SUBS, LANES), 0)
    odd = row % 2 == 1
    decay_64 = decay_32 * decay_32
    decay_128 = decay_64 * decay_64
    first = jnp.where(core == 0, near, far)
    second = jnp.where(core == 0, far, near)
    first_before, second_before = pltpu.roll(first, 1, 0), pltpu.roll(second, 1, 0)
    first_whole = first + decay_32 * first_before
    held = second + decay_32 * second_before + decay_64 * first_whole
    held = held + decay_128 * jnp.where(row >= 2, pltpu.roll(held, 2, 0), 0.0)
    held = held + decay_128 * decay_128 * jnp.where(row >= 4, pltpu.roll(held, 4, 0), 0.0)
    into = jnp.where(odd, pltpu.roll(held, 2, 0), pltpu.roll(held, 1, 0))
    into = jnp.where(row >= 2, into, 0.0)
    middle = decay_64 * into + jnp.where(odd, first_whole, pltpu.roll(first_whole, SUBS - 1, 0))
    first = jnp.where(odd, decay_32 * into + first_before, into)
    second = jnp.where(odd, decay_32 * middle + second_before, middle)
    return jnp.where(core == 0, first, second), jnp.where(core == 0, second, first)


def local_kernel(modes, begin, *refs):
    drive_refs, (near_ref, far_ref, decay_ref, step_decay_ref, weight_ref, skip_ref), out_refs = refs[:2], refs[2:8], refs[8:]
    groups, tokens, _ = out_refs[0].shape
    steps = tokens // SUBS
    core = lax.axis_index("tp") % 2
    for group in range(groups):
        lanes = pl.ds((begin + group) * LANES, LANES)
        decay = [wide(decay_ref, mode, lanes) for mode in range(modes)]
        weight = [wide(weight_ref, mode, lanes) for mode in range(modes)]
        skip = jnp.broadcast_to(skip_ref[0:1, lanes], (SUBS, LANES))
        starts = [
            first_states(near_ref[m, :, lanes], far_ref[m, :, lanes], wide(step_decay_ref, m, lanes), core)
            for m in range(modes)
        ]
        for part, (drive_ref, out_ref) in enumerate(zip(drive_refs, out_refs)):

            def step(i, states):
                at = pl.ds(pl.multiple_of(i * SUBS, SUBS), SUBS)
                x = drive_ref[begin + group, at, :]
                states = [states[m] * decay[m] + x for m in range(modes)]
                out_ref[group, at, :] = total_of([states[m] * weight[m] for m in range(modes)] + [skip * x])
                return states

            lax.fori_loop(0, steps, step, [start[part] for start in starts], unroll=8)


def final_kernel(modes, early, *refs):
    row = lax.axis_index("ctx") // 4

    @pl.when(row == 0 if early else row > 0)
    def _():
        finish(modes, *refs[: 9], *refs[9 if early else 10 :])


def finish(modes, *refs):
    low_refs, high_refs = refs[0:2], refs[2:4]
    query_ref, carry_ref, near_ref, far_ref, decay_ref, out_ref, sum_ref, held_ref, out_sem = refs[4:]
    groups, tokens = sum_ref.shape[1], low_refs[0].shape[1]
    steps = tokens // SUBS
    core = lax.axis_index("tp") % 2

    def copy_out(group):
        return pltpu.make_async_copy(held_ref.at[group], out_ref.at[pl.ds(group * LANES, LANES)], out_sem.at[group])

    for group in range(groups):
        lanes = pl.ds(group * LANES, LANES)
        decay = [wide(decay_ref, mode, lanes) for mode in range(modes)]
        local_refs = low_refs if group < groups // 2 else high_refs
        for part, start_ref in enumerate((near_ref, far_ref)):
            local_ref = local_refs[part]
            first = [start_ref[mode, :, lanes] * wide(carry_ref, mode, lanes) for mode in range(modes)]

            def step(i, states):
                at = pl.ds(pl.multiple_of(i * SUBS, SUBS), SUBS)
                sum_ref[core ^ part, group, at, :] = total_of([local_ref[group % (groups // 2), at, :]] + states)
                return [states[m] * decay[m] for m in range(modes)]

            lax.fori_loop(0, steps, step, first, unroll=steps)
        for tile in range(2 * tokens // LANES):
            rows = pl.ds(tile * LANES, LANES)
            subs = [sum_ref[part, group, pl.ds(2 * tile + j, steps, stride=SUBS), :] for part in range(2) for j in range(2)]
            mixed = jnp.concatenate(subs)
            gated = mixed * query_ref[rows, lanes].astype(F32)
            held_ref[group, :, rows] = gated.T.astype(BF16)
        copy_out(group).start()
    for group in range(groups):
        copy_out(group).wait()


def per_device(qkv, residues, spans, skip):
    _, span_tokens, _ = qkv.shape
    devices = lax.axis_size("tp")
    chips = devices // 2
    channels, modes = residues.shape
    tokens = devices * span_tokens
    half = tokens // 2
    groups = channels // LANES
    steps = half // SUBS
    core = lax.axis_index("tp") % 2

    code = list(
        pl.pallas_call(
            open_kernel,
            in_specs=[pl.BlockSpec(memory_space=pl.ANY)],
            out_specs=[VMEM] * chips,
            out_shape=[jax.ShapeDtypeStruct((2, span_tokens, channels), BF16)] * chips,
            scratch_shapes=[
                pltpu.VMEM((chips, 2, span_tokens, 2 * channels), BF16),
                pltpu.SemaphoreType.DMA((chips,)),
            ],
            compiler_params=pltpu.CompilerParams(vmem_limit_bytes=OPEN_VMEM),
        )(qkv)
    )
    query = pl.pallas_call(
        query_kernel,
        in_specs=[VMEM],
        out_specs=pl.BlockSpec(memory_space=pl.ANY),
        out_shape=jax.ShapeDtypeStruct((devices, span_tokens, channels), BF16),
        scratch_shapes=[pltpu.VMEM((devices, span_tokens, channels), BF16), pltpu.SemaphoreType.DMA((devices,))],
        compiler_params=PARAMS,
    )(qkv)
    for k in CHIP_ORDER:
        code[k] = across_chips(code[k], k)
    query = lax.all_to_all(query, "tp", 0, 0).reshape(tokens, channels)
    code = [code[0]] + [code[k] for k in CHIP_ORDER]
    near_code = jnp.stack([piece[0] for piece in code])
    far_code = across_core(jnp.stack([piece[1] for piece in code]))

    rates = 1.0 / spans.T
    weight = residues.T * jnp.sqrt(rates) * (1.0 / SCALE)
    decay = jnp.exp(-rates)
    sub_index = jnp.arange(SUBS, dtype=jnp.int32)

    def first_token(side):
        return (2 * span_tokens * (sub_index // 2) + steps * (sub_index % 2) + span_tokens * side).astype(F32)[None, :, None]

    def tail(side):
        return jnp.exp(-rates[:, None, :] * (tokens - steps - first_token(side)))

    def start(side):
        return weight[:, None, :] * jnp.exp(-rates[:, None, :] * (first_token(side) + 1.0))

    def states(code, tail, earlier):
        return pl.pallas_call(
            functools.partial(state_kernel, modes),
            in_specs=[VMEM] * 4,
            out_specs=[VMEM] * 3,
            out_shape=[
                jax.ShapeDtypeStruct((groups, half + SUBS, LANES), F32),
                jax.ShapeDtypeStruct((modes, SUBS, channels), F32),
                jax.ShapeDtypeStruct((modes, channels), F32),
            ],
            compiler_params=PARAMS,
            cost_estimate=pl.CostEstimate(flops=1000, bytes_accessed=1000, transcendentals=0),
        )(code, decay, tail, earlier)

    near_drive, near_subs, block = states(near_code, tail(core), jnp.zeros((modes, channels), F32))
    far_drive, far_subs, block = states(far_code, tail(1 - core), block)
    rates, weight, block = lax.optimization_barrier((rates, weight, block))
    step_decay = jnp.exp(-rates * steps)

    local = [
        pl.pallas_call(
            functools.partial(local_kernel, modes, begin),
            in_specs=[VMEM] * 8,
            out_specs=[VMEM] * 2,
            out_shape=[jax.ShapeDtypeStruct((groups // 2, half, LANES), F32)] * 2,
            compiler_params=PARAMS,
            cost_estimate=pl.CostEstimate(flops=40_000_000, bytes_accessed=4_000_000, transcendentals=0),
        )(
            near_drive, far_drive, near_subs, far_subs, decay, step_decay, weight,
            skip.reshape(1, channels) * (1.0 / SCALE),
        )
        for begin in (0, groups // 2)
    ]

    index = lax.axis_index("ctx")
    col, row = index % 4, index // 4

    def power(count):
        count = jnp.asarray(count)
        return jnp.where(count >= 0, jnp.exp(-rates * jnp.maximum(count, 0).astype(F32)), 0.0)

    near_start, far_start = start(core), start(1 - core)

    def final(carry, out=None):
        early = out is None
        return pl.pallas_call(
            functools.partial(final_kernel, modes, early),
            in_specs=[VMEM] * 9 + [pl.BlockSpec(memory_space=pl.ANY)] * (not early),
            out_specs=pl.BlockSpec(memory_space=pl.ANY),
            out_shape=jax.ShapeDtypeStruct((channels, tokens), BF16),
            input_output_aliases={} if early else {9: 0},
            scratch_shapes=[
                pltpu.VMEM((2, groups, half + SUBS, LANES), F32),
                pltpu.VMEM((groups, LANES, tokens), BF16),
                pltpu.SemaphoreType.DMA((groups,)),
            ],
            compiler_params=PARAMS,
        )(*local[0], *local[1], query, carry, near_start, far_start, decay, *(() if early else (out,)))

    others = [across_blocks(block, k) for k in COL_ORDER]
    others, query, local = lax.optimization_barrier((others, query, local))
    before = jnp.zeros_like(block)
    total = power(tokens * (3 - col)) * block
    for k, other in zip(COL_ORDER, others):
        before = before + power(tokens * (col - 1 - (col ^ k))) * other
        total = total + power(tokens * (3 - (col ^ k))) * other
    others = [across_blocks(total, 4 * k) for k in ROW_ORDER]
    others, out = lax.optimization_barrier((others, final(before)))
    carry = jnp.zeros_like(block)
    for k, other in zip(ROW_ORDER, others):
        carry = carry + power(4 * tokens * (row - 1 - (row ^ k))) * other
    return final(before + power(tokens * col) * carry, out)


def solution(mesh):
    return jax.shard_map(
        per_device,
        mesh=mesh,
        in_specs=(P(None, ("ctx", "tp"), None), P("tp", None), P("tp", None), P("tp")),
        out_specs=P("tp", "ctx"),
        check_vma=False,
    )
```

```python
import functools

import jax
import jax.numpy as jnp
from jax import lax
from jax.experimental import pallas as pl
from jax.experimental.pallas import tpu as pltpu
from jax.sharding import PartitionSpec as P

F32 = jnp.float32
BF16 = jnp.bfloat16
SUBS = 8
LANES = 128
SCALE = 1024.0
OPEN_VMEM = 52 * 1024 * 1024
CHIP_ORDER = (2, 1, 3)
COL_ORDER = (3, 2, 1)
ROW_ORDER = (2, 3, 1)
VMEM = pl.BlockSpec(memory_space=pltpu.VMEM)
PARAMS = pltpu.CompilerParams(vmem_limit_bytes=32 * 1024 * 1024)


def encode(scaled):
    size = jnp.maximum(jnp.abs(scaled), 1.0)
    square = size * size
    return (scaled * (square * square * square * size)).astype(BF16)


def decode(code):
    code = code.astype(F32)
    half = lax.rsqrt(jnp.maximum(jnp.abs(code), 1.0))
    eighth = lax.rsqrt(lax.rsqrt(half))
    return code * (half * eighth * eighth * eighth)


def open_kernel(qkv_ref, *refs):
    *code_refs, held_ref, held_sem = refs
    _, _, width = code_refs[0].shape
    place = lax.axis_index("tp")

    def fetch(k):
        lanes = pl.ds(pl.multiple_of((place // 2 ^ k) * 2 * width, 2 * width), 2 * width)
        return pltpu.make_async_copy(qkv_ref.at[pl.ds(1, 2), :, lanes], held_ref.at[k], held_sem.at[k])

    order = CHIP_ORDER + (0,)
    for k in order:
        fetch(k).start()
    for k in order:
        fetch(k).wait()
        for flip in range(2):
            half = pl.ds(pl.multiple_of((place % 2 ^ flip) * width, width), width)
            scaled = held_ref[k, 0, :, half].astype(F32) * held_ref[k, 1, :, half].astype(F32) * SCALE
            code_refs[k][flip] = encode(scaled)


def query_kernel(qkv_ref, query_ref, moved_ref, sem):
    parts, _, width = moved_ref.shape
    copies = [pltpu.make_async_copy(moved_ref.at[part], query_ref.at[part], sem.at[part]) for part in range(parts)]
    for part in range(parts):
        moved_ref[part] = qkv_ref[0, :, pl.ds(part * width, width)]
        copies[part].start()
    for copy in copies:
        copy.wait()


def across_core(value):
    return lax.ppermute(value, "tp", [(i, i ^ 1) for i in range(lax.axis_size("tp"))])


def across_chips(value, k):
    return lax.ppermute(value, "tp", [(i, i ^ 2 * k) for i in range(lax.axis_size("tp"))])


def across_blocks(value, bits):
    return lax.ppermute(value, "ctx", [(i, i ^ bits) for i in range(lax.axis_size("ctx"))])


def wide(ref, mode, lanes):
    return jnp.broadcast_to(ref[mode : mode + 1, lanes], (SUBS, LANES))


def total_of(parts):
    while len(parts) > 1:
        parts = [parts[j] + parts[j + 1] if j + 1 < len(parts) else parts[j] for j in range(0, len(parts), 2)]
    return parts[0]


def state_kernel(modes, code_ref, decay_ref, tail_ref, earlier_ref, drive_ref, sub_ref, block_ref):
    chips, tokens, channels = code_ref.shape
    steps = chips * tokens // SUBS
    chip = lax.axis_index("tp") // 2
    for source in range(chips):
        k = chip ^ source
        slot = k % 2 * 2 + k // 2
        for group in range(channels // LANES):
            lanes = pl.ds(group * LANES, LANES)
            drive = decode(code_ref[slot, :, lanes])
            for sub in range(SUBS * source // chips, SUBS * (source + 1) // chips):
                at = sub * steps - source * tokens
                drive_ref[group, pl.ds(sub, steps, stride=SUBS), :] = drive[at : at + steps]
    for group in range(channels // LANES):
        lanes = pl.ds(group * LANES, LANES)
        decay = [wide(decay_ref, mode, lanes) for mode in range(modes)]

        def step(i, states):
            x = drive_ref[group, pl.ds(pl.multiple_of(i * SUBS, SUBS), SUBS), :]
            return [states[m] * decay[m] + x for m in range(modes)]

        zero = jnp.zeros((SUBS, LANES), F32)
        states = lax.fori_loop(0, steps, step, [zero] * modes, unroll=steps)
        for mode in range(modes):
            sub_ref[mode, :, lanes] = states[mode]
            block_ref[mode : mode + 1, lanes] = earlier_ref[mode : mode + 1, lanes] + jnp.sum(
                states[mode] * tail_ref[mode, :, lanes], axis=0, keepdims=True
            )


def first_states(near, far, decay_32, core):
    row = lax.broadcasted_iota(jnp.int32, (SUBS, LANES), 0)
    odd = row % 2 == 1
    decay_64 = decay_32 * decay_32
    decay_128 = decay_64 * decay_64
    first = jnp.where(core == 0, near, far)
    second = jnp.where(core == 0, far, near)
    first_before, second_before = pltpu.roll(first, 1, 0), pltpu.roll(second, 1, 0)
    first_whole = first + decay_32 * first_before
    held = second + decay_32 * second_before + decay_64 * first_whole
    held = held + decay_128 * jnp.where(row >= 2, pltpu.roll(held, 2, 0), 0.0)
    held = held + decay_128 * decay_128 * jnp.where(row >= 4, pltpu.roll(held, 4, 0), 0.0)
    into = jnp.where(odd, pltpu.roll(held, 2, 0), pltpu.roll(held, 1, 0))
    into = jnp.where(row >= 2, into, 0.0)
    middle = decay_64 * into + jnp.where(odd, first_whole, pltpu.roll(first_whole, SUBS - 1, 0))
    first = jnp.where(odd, decay_32 * into + first_before, into)
    second = jnp.where(odd, decay_32 * middle + second_before, middle)
    return jnp.where(core == 0, first, second), jnp.where(core == 0, second, first)


def local_kernel(modes, begin, *refs):
    drive_refs, (near_ref, far_ref, decay_ref, step_decay_ref, weight_ref, skip_ref), out_refs = refs[:2], refs[2:8], refs[8:]
    groups, tokens, _ = out_refs[0].shape
    steps = tokens // SUBS
    core = lax.axis_index("tp") % 2
    for group in range(groups):
        lanes = pl.ds((begin + group) * LANES, LANES)
        decay = [wide(decay_ref, mode, lanes) for mode in range(modes)]
        weight = [wide(weight_ref, mode, lanes) for mode in range(modes)]
        skip = jnp.broadcast_to(skip_ref[0:1, lanes], (SUBS, LANES))
        starts = [
            first_states(near_ref[m, :, lanes], far_ref[m, :, lanes], wide(step_decay_ref, m, lanes), core)
            for m in range(modes)
        ]
        for part, (drive_ref, out_ref) in enumerate(zip(drive_refs, out_refs)):

            def step(i, states):
                at = pl.ds(pl.multiple_of(i * SUBS, SUBS), SUBS)
                x = drive_ref[begin + group, at, :]
                states = [states[m] * decay[m] + x for m in range(modes)]
                out_ref[group, at, :] = total_of([states[m] * weight[m] for m in range(modes)] + [skip * x])
                return states

            lax.fori_loop(0, steps, step, [start[part] for start in starts], unroll=8)


def final_kernel(modes, early, *refs):
    row = lax.axis_index("ctx") // 4

    @pl.when(row == 0 if early else row > 0)
    def _():
        finish(modes, *refs[: 9], *refs[9 if early else 10 :])


def finish(modes, *refs):
    low_refs, high_refs = refs[0:2], refs[2:4]
    query_ref, carry_ref, near_ref, far_ref, decay_ref, out_ref, sum_ref, held_ref, out_sem = refs[4:]
    groups, tokens = sum_ref.shape[1], low_refs[0].shape[1]
    steps = tokens // SUBS
    core = lax.axis_index("tp") % 2

    def copy_out(group):
        return pltpu.make_async_copy(held_ref.at[group], out_ref.at[pl.ds(group * LANES, LANES)], out_sem.at[group])

    for group in range(groups):
        lanes = pl.ds(group * LANES, LANES)
        decay = [wide(decay_ref, mode, lanes) for mode in range(modes)]
        local_refs = low_refs if group < groups // 2 else high_refs
        for part, start_ref in enumerate((near_ref, far_ref)):
            local_ref = local_refs[part]
            first = [start_ref[mode, :, lanes] * wide(carry_ref, mode, lanes) for mode in range(modes)]

            def step(i, states):
                at = pl.ds(pl.multiple_of(i * SUBS, SUBS), SUBS)
                sum_ref[core ^ part, group, at, :] = total_of([local_ref[group % (groups // 2), at, :]] + states)
                return [states[m] * decay[m] for m in range(modes)]

            lax.fori_loop(0, steps, step, first, unroll=steps)
        for tile in range(2 * tokens // LANES):
            rows = pl.ds(tile * LANES, LANES)
            subs = [sum_ref[part, group, pl.ds(2 * tile + j, steps, stride=SUBS), :] for part in range(2) for j in range(2)]
            mixed = jnp.concatenate(subs)
            gated = mixed * query_ref[rows, lanes].astype(F32)
            held_ref[group, :, rows] = gated.T.astype(BF16)
        copy_out(group).start()
    for group in range(groups):
        copy_out(group).wait()


def per_device(qkv, residues, spans, skip):
    _, span_tokens, _ = qkv.shape
    devices = lax.axis_size("tp")
    chips = devices // 2
    channels, modes = residues.shape
    tokens = devices * span_tokens
    half = tokens // 2
    groups = channels // LANES
    steps = half // SUBS
    core = lax.axis_index("tp") % 2

    code = list(
        pl.pallas_call(
            open_kernel,
            in_specs=[pl.BlockSpec(memory_space=pl.ANY)],
            out_specs=[VMEM] * chips,
            out_shape=[jax.ShapeDtypeStruct((2, span_tokens, channels), BF16)] * chips,
            scratch_shapes=[
                pltpu.VMEM((chips, 2, span_tokens, 2 * channels), BF16),
                pltpu.SemaphoreType.DMA((chips,)),
            ],
            compiler_params=pltpu.CompilerParams(vmem_limit_bytes=OPEN_VMEM),
        )(qkv)
    )
    query = pl.pallas_call(
        query_kernel,
        in_specs=[VMEM],
        out_specs=pl.BlockSpec(memory_space=pl.ANY),
        out_shape=jax.ShapeDtypeStruct((devices, span_tokens, channels), BF16),
        scratch_shapes=[pltpu.VMEM((devices, span_tokens, channels), BF16), pltpu.SemaphoreType.DMA((devices,))],
        compiler_params=PARAMS,
    )(qkv)
    for k in CHIP_ORDER:
        code[k] = across_chips(code[k], k)
    query = lax.all_to_all(query, "tp", 0, 0).reshape(tokens, channels)
    code = [code[0]] + [code[k] for k in CHIP_ORDER]
    near_code = jnp.stack([piece[0] for piece in code])
    far_code = across_core(jnp.stack([piece[1] for piece in code]))

    rates = 1.0 / spans.T
    weight = residues.T * jnp.sqrt(rates) * (1.0 / SCALE)
    decay = jnp.exp(-rates)
    sub_index = jnp.arange(SUBS, dtype=jnp.int32)

    def first_token(side):
        return (2 * span_tokens * (sub_index // 2) + steps * (sub_index % 2) + span_tokens * side).astype(F32)[None, :, None]

    def tail(side):
        return jnp.exp(-rates[:, None, :] * (tokens - steps - first_token(side)))

    def start(side):
        return weight[:, None, :] * jnp.exp(-rates[:, None, :] * (first_token(side) + 1.0))

    def states(code, tail, earlier):
        return pl.pallas_call(
            functools.partial(state_kernel, modes),
            in_specs=[VMEM] * 4,
            out_specs=[VMEM] * 3,
            out_shape=[
                jax.ShapeDtypeStruct((groups, half + SUBS, LANES), F32),
                jax.ShapeDtypeStruct((modes, SUBS, channels), F32),
                jax.ShapeDtypeStruct((modes, channels), F32),
            ],
            compiler_params=PARAMS,
            cost_estimate=pl.CostEstimate(flops=1000, bytes_accessed=1000, transcendentals=0),
        )(code, decay, tail, earlier)

    near_drive, near_subs, block = states(near_code, tail(core), jnp.zeros((modes, channels), F32))
    far_drive, far_subs, block = states(far_code, tail(1 - core), block)
    rates, weight, block = lax.optimization_barrier((rates, weight, block))
    step_decay = jnp.exp(-rates * steps)

    local = [
        pl.pallas_call(
            functools.partial(local_kernel, modes, begin),
            in_specs=[VMEM] * 8,
            out_specs=[VMEM] * 2,
            out_shape=[jax.ShapeDtypeStruct((groups // 2, half, LANES), F32)] * 2,
            compiler_params=PARAMS,
            cost_estimate=pl.CostEstimate(flops=40_000_000, bytes_accessed=4_000_000, transcendentals=0),
        )(
            near_drive, far_drive, near_subs, far_subs, decay, step_decay, weight,
            skip.reshape(1, channels) * (1.0 / SCALE),
        )
        for begin in (0, groups // 2)
    ]

    index = lax.axis_index("ctx")
    col, row = index % 4, index // 4

    def power(count):
        count = jnp.asarray(count)
        return jnp.where(count >= 0, jnp.exp(-rates * jnp.maximum(count, 0).astype(F32)), 0.0)

    near_start, far_start = start(core), start(1 - core)

    def final(carry, out=None):
        early = out is None
        return pl.pallas_call(
            functools.partial(final_kernel, modes, early),
            in_specs=[VMEM] * 9 + [pl.BlockSpec(memory_space=pl.ANY)] * (not early),
            out_specs=pl.BlockSpec(memory_space=pl.ANY),
            out_shape=jax.ShapeDtypeStruct((channels, tokens), BF16),
            input_output_aliases={} if early else {9: 0},
            scratch_shapes=[
                pltpu.VMEM((2, groups, half + SUBS, LANES), F32),
                pltpu.VMEM((groups, LANES, tokens), BF16),
                pltpu.SemaphoreType.DMA((groups,)),
            ],
            compiler_params=PARAMS,
        )(*local[0], *local[1], query, carry, near_start, far_start, decay, *(() if early else (out,)))

    others = [across_blocks(block, k) for k in COL_ORDER]
    others, query, local = lax.optimization_barrier((others, query, local))
    before = jnp.zeros_like(block)
    total = power(tokens * (3 - col)) * block
    for k, other in zip(COL_ORDER, others):
        before = before + power(tokens * (col - 1 - (col ^ k))) * other
        total = total + power(tokens * (3 - (col ^ k))) * other
    others = [across_blocks(total, 4 * k) for k in ROW_ORDER]
    others, out = lax.optimization_barrier((others, final(before)))
    carry = jnp.zeros_like(block)
    for k, other in zip(ROW_ORDER, others):
        carry = carry + power(4 * tokens * (row - 1 - (row ^ k))) * other
    return final(before + power(tokens * col) * carry, out)


def solution(mesh):
    return jax.shard_map(
        per_device,
        mesh=mesh,
        in_specs=(P(None, ("ctx", "tp"), None), P("tp", None), P("tp", None), P("tp")),
        out_specs=P("tp", "ctx"),
        check_vma=False,
    )
```
